32 devices in a mesh: dp: 16 (over z, y, core), fsdp: 2 (over x).
Axes of the slice: x: 2, y: 2, z: 4, core: 2. Of those that a mesh axis runs over, the one named last changes fastest.
Arguments:
- tokens: bfloat16 [32, 2, 128, 1024], P(('dp', 'fsdp')), may hold values from -6 to 6
- encoded: bfloat16 [32, 512, 1024], P(('dp', 'fsdp')), may hold values from -6 to 6
- cotangent: bfloat16 [32, 2, 128, 1024], P(('dp', 'fsdp')), may hold values from -12 to 12
- buckets: int32 [32, 2, 128, 256], P(('dp', 'fsdp')), may hold values from 0 to 31
- lengths: int32 [32], P(('dp', 'fsdp')), may hold values from 32 to 128, as said below
- self_q: bfloat16 [1024, 1024], P(('dp', 'fsdp')), may hold values from -0.1875 to 0.1875
- self_qb: bfloat16 [1024], P(('dp', 'fsdp')), may hold values from -1.75 to 1.75
- self_k: bfloat16 [1024, 1024], P(('dp', 'fsdp')), may hold values from -0.1875 to 0.1875
- self_v: bfloat16 [1024, 1024], P(('dp', 'fsdp')), may hold values from -0.1875 to 0.1875
- self_vb: bfloat16 [1024], P(('dp', 'fsdp')), may hold values from -1.75 to 1.75
- self_o: bfloat16 [1024, 1024], P(('dp', 'fsdp')), may hold values from -0.75 to 0.75
- self_ob: bfloat16 [1024], P(('dp', 'fsdp')), may hold values from -1.75 to 1.75
- bucket_w: bfloat16 [1024, 512], P(('dp', 'fsdp')), may hold values from -0.1875 to 0.1875
- bucket_b: bfloat16 [512], P(('dp', 'fsdp')), may hold values from -3 to 3
- cross_q: bfloat16 [1024, 1024], P(('dp', 'fsdp')), may hold values from -0.1875 to 0.1875
- cross_qb: bfloat16 [1024], P(('dp', 'fsdp')), may hold values from -1.75 to 1.75
- cross_k: bfloat16 [1024, 1024], P(('dp', 'fsdp')), may hold values from -0.1875 to 0.1875
- cross_v: bfloat16 [1024, 1024], P(('dp', 'fsdp')), may hold values from -0.1875 to 0.1875
- cross_vb: bfloat16 [1024], P(('dp', 'fsdp')), may hold values from -1.75 to 1.75
- cross_o: bfloat16 [1024, 1024], P(('dp', 'fsdp')), may hold values from -1 to 1
- cross_ob: bfloat16 [1024], P(('dp', 'fsdp')), may hold values from -1.75 to 1.75
- ffn_in: bfloat16 [1024, 4096], P(('dp', 'fsdp')), may hold values from -0.1875 to 0.1875
- ffn_inb: bfloat16 [4096], P(('dp', 'fsdp')), may hold values from -1.75 to 1.75
- ffn_out: bfloat16 [4096, 1024], P(('dp', 'fsdp')), may hold values from -0.125 to 0.125
- ffn_outb: bfloat16 [1024], P(('dp', 'fsdp')), may hold values from -1.75 to 1.75
- gain_a: bfloat16 [1024], P(('dp', 'fsdp')), may hold values from 0.5 to 1.5
- shift_a: bfloat16 [1024], P(('dp', 'fsdp')), may hold values from -1.75 to 1.75
- gain_b: bfloat16 [1024], P(('dp', 'fsdp')), may hold values from 0.5 to 1.5
- shift_b: bfloat16 [1024], P(('dp', 'fsdp')), may hold values from -1.75 to 1.75
- gain_c: bfloat16 [1024], P(('dp', 'fsdp')), may hold values from 0.5 to 1.5
- shift_c: bfloat16 [1024], P(('dp', 'fsdp')), may hold values from -1.75 to 1.75
Outputs:
- outputs: bfloat16 [32, 2, 128, 1024], P(('dp', 'fsdp'))
- grad_tokens: float32 [32, 2, 128, 1024], P(('dp', 'fsdp'))
- grad_encoded: float32 [32, 512, 1024], P(('dp', 'fsdp'))
- grad_self_q: float32 [1024, 1024], P(('dp', 'fsdp'))
- grad_self_qb: float32 [1024], P(('dp', 'fsdp'))
- grad_self_k: float32 [1024, 1024], P(('dp', 'fsdp'))
- grad_self_v: float32 [1024, 1024], P(('dp', 'fsdp'))
- grad_self_vb: float32 [1024], P(('dp', 'fsdp'))
- grad_self_o: float32 [1024, 1024], P(('dp', 'fsdp'))
- grad_self_ob: float32 [1024], P(('dp', 'fsdp'))
- grad_bucket_w: float32 [1024, 512], P(('dp', 'fsdp'))
- grad_bucket_b: float32 [512], P(('dp', 'fsdp'))
- grad_cross_q: float32 [1024, 1024], P(('dp', 'fsdp'))
- grad_cross_qb: float32 [1024], P(('dp', 'fsdp'))
- grad_cross_k: float32 [1024, 1024], P(('dp', 'fsdp'))
- grad_cross_v: float32 [1024, 1024], P(('dp', 'fsdp'))
- grad_cross_vb: float32 [1024], P(('dp', 'fsdp'))
- grad_cross_o: float32 [1024, 1024], P(('dp', 'fsdp'))
- grad_cross_ob: float32 [1024], P(('dp', 'fsdp'))
- grad_ffn_in: float32 [1024, 4096], P(('dp', 'fsdp'))
- grad_ffn_inb: float32 [4096], P(('dp', 'fsdp'))
- grad_ffn_out: float32 [4096, 1024], P(('dp', 'fsdp'))
- grad_ffn_outb: float32 [1024], P(('dp', 'fsdp'))
- grad_gain_a: float32 [1024], P(('dp', 'fsdp'))
- grad_shift_a: float32 [1024], P(('dp', 'fsdp'))
- grad_gain_b: float32 [1024], P(('dp', 'fsdp'))
- grad_shift_b: float32 [1024], P(('dp', 'fsdp'))
- grad_gain_c: float32 [1024], P(('dp', 'fsdp'))
- grad_shift_c: float32 [1024], P(('dp', 'fsdp'))
The draws below stay inside these ranges and needn't reach their ends.
Inputs may be any that keep to these rules, and one draw needn't show every extreme that they name: Target lengths; some item has 128 and some item has 32.
All inputs are finite; a program needn't handle non-finite values.
Results may differ from the reference program's by a relative error of at most 0.023.
Values may be sent and summed in bfloat16 or wider, within the bound.
A program may use at most 320 MiB of HBM per device.

```python
import jax
import jax.numpy as jnp
from jax import lax

D = 1024
HEADS = 16
HEAD_DIM = 64
FF = 4096
BUCKETS = 32
TGT = 128
SRC = 512
ITEMS = 32


def draw_lengths(key, part):
    key = jax.random.fold_in(key, 7)
    drawn = jax.random.randint(key, (ITEMS,), TGT // 4, TGT + 1, dtype=jnp.int32)
    drawn = drawn.at[0].set(TGT)
    return drawn.at[1].set(TGT // 4)


def plant(values, key, low, top_value):
    shape = values.shape
    spot = [jax.random.randint(jax.random.fold_in(key, axis), (), 0, shape[axis]) for axis in range(len(shape))]
    values = values.at[tuple(spot)].set(low)
    longest = shape.index(max(shape))
    spot[longest] = (spot[longest] + 1) % shape[longest]
    return values.at[tuple(spot)].set(top_value)


def strengthened(array, key, source, target, parts, factor):
    owner, partner = [(jnp.arange(array.shape[position]) // (array.shape[position] // parts)).reshape([-1 if axis == position else 1 for axis in range(array.ndim)]) for position in (source, target)]
    chosen = jax.random.permutation(key, parts)[partner]
    strong = (owner == chosen) | (owner == (partner + parts // 2) % parts)
    return jnp.where(strong, factor * array, array)


def block_scale(own_key, extent, split, low, high):
    def one(position, blocks):
        draws = jax.random.uniform(jax.random.fold_in(jax.random.fold_in(own_key, 6), position), (blocks,), jnp.float32, low / len(split), high / len(split))
        return jnp.repeat(jnp.exp(draws), extent[position] // blocks).reshape((-1,) + (1,) * (len(extent) - position - 1))

    level = one(*split[0])
    for cut in split[1:]:
        level = level * one(*cut)
    return level


def normal_values(key, shape, scale, most, pieces=(), kind=jnp.bfloat16):
    entries = jax.random.normal(key, shape, jnp.float32) * scale
    if len(pieces) > 0:
        entries = block_scale(key, shape, pieces, -0.22, 0.18) * entries
    return jnp.clip(entries, min=-most, max=most).astype(kind)


def noise_with(rng, extent, width, reach, cuts, heavy, kind=jnp.bfloat16):
    array = width * jax.random.normal(rng, extent, jnp.float32)
    if cuts:
        array = array * block_scale(rng, extent, cuts, -0.22, 0.18)
    return jnp.clip(strengthened(array, jax.random.fold_in(rng, 3), *heavy), -reach, reach).astype(kind)


def setup_inputs(seed: int = 0) -> dict:
    key_of = jax.random.split(jax.random.key(seed), 32)
    return {
        "tokens": normal_values(key_of[0], (ITEMS, 2, TGT, D), 1.0, 6.0, ((0, 32),)),
        "encoded": normal_values(key_of[1], (ITEMS, SRC, D), 1.0, 6.0, ((0, 32),)),
        "cotangent": noise_with(key_of[2], (ITEMS, 2, TGT, D), 1.0, 12.0, ((0, 32),), (0, 3, 32, 2.75)),
        "buckets": plant(jax.random.randint(key_of[3], (ITEMS, 2, TGT, 2 * TGT), 0, BUCKETS), jax.random.fold_in(key_of[3], 1), 0, BUCKETS - 1).astype(jnp.int32),
        "lengths": draw_lengths(jax.random.fold_in(key_of[31], 71), 0),
        "self_q": normal_values(key_of[5], (D, D), D ** -0.5, 0.1875, ((0, 32),)),
        "self_qb": normal_values(key_of[6], (D,), 0.3, 1.75, ((0, 32),)),
        "self_k": normal_values(key_of[7], (D, D), D ** -0.5, 0.1875, ((0, 32),)),
        "self_v": normal_values(key_of[8], (D, D), D ** -0.5, 0.1875, ((0, 32),)),
        "self_vb": normal_values(key_of[9], (D,), 0.3, 1.75, ((0, 32),)),
        "self_o": normal_values(key_of[10], (D, D), (D // 16) ** -0.5, 0.75, ((0, 32),)),
        "self_ob": normal_values(key_of[11], (D,), 0.3, 1.75, ((0, 32),)),
        "bucket_w": normal_values(key_of[12], (D, BUCKETS * HEADS), D ** -0.5, 0.1875, ((0, 32),)),
        "bucket_b": normal_values(key_of[13], (BUCKETS * HEADS,), 0.5, 3.0, ((0, 32),)),
        "cross_q": normal_values(key_of[14], (D, D), D ** -0.5, 0.1875, ((0, 32),)),
        "cross_qb": normal_values(key_of[15], (D,), 0.3, 1.75, ((0, 32),)),
        "cross_k": normal_values(key_of[16], (D, D), D ** -0.5, 0.1875, ((0, 32),)),
        "cross_v": normal_values(key_of[17], (D, D), D ** -0.5, 0.1875, ((0, 32),)),
        "cross_vb": normal_values(key_of[18], (D,), 0.3, 1.75, ((0, 32),)),
        "cross_o": normal_values(key_of[19], (D, D), (D // 32) ** -0.5, 1.0, ((0, 32),)),
        "cross_ob": normal_values(key_of[20], (D,), 0.3, 1.75, ((0, 32),)),
        "ffn_in": normal_values(key_of[21], (D, FF), D ** -0.5, 0.1875, ((0, 32),)),
        "ffn_inb": normal_values(key_of[22], (FF,), 0.3, 1.75, ((0, 32),)),
        "ffn_out": normal_values(key_of[23], (FF, D), (FF // 2) ** -0.5, 0.125, ((0, 32),)),
        "ffn_outb": normal_values(key_of[24], (D,), 0.3, 1.75, ((0, 32),)),
        "gain_a": jnp.clip(1.0 + 0.1 * jax.random.normal(key_of[25], (D,), jnp.float32), 0.5, 1.5).astype(jnp.bfloat16),
        "shift_a": normal_values(key_of[26], (D,), 0.3, 1.75, ((0, 32),)),
        "gain_b": jnp.clip(1.0 + 0.1 * jax.random.normal(key_of[27], (D,), jnp.float32), 0.5, 1.5).astype(jnp.bfloat16),
        "shift_b": normal_values(key_of[28], (D,), 0.3, 1.75, ((0, 32),)),
        "gain_c": jnp.clip(1.0 + 0.1 * jax.random.normal(key_of[29], (D,), jnp.float32), 0.5, 1.5).astype(jnp.bfloat16),
        "shift_c": normal_values(key_of[30], (D,), 0.3, 1.75, ((0, 32),)),
    }


@jax.custom_vjp
def low(v):
    return lax.optimization_barrier(v.astype(jnp.bfloat16)).astype(jnp.float32)

@jax.custom_vjp
def low_back(v):
    return v

def low_keep(v):
    return (low(v), None)

def low_pass(kept, grad):
    return (grad,)

def back_keep(v):
    return (v, None)

def back_low(kept, grad):
    return (low(grad),)
low.defvjp(low_keep, low_pass)
low_back.defvjp(back_keep, back_low)

def matmul(left, right):
    return jnp.dot(left, right, precision=lax.Precision.HIGHEST)

def layer_norm(summed, gain, shift):
    center = summed - lax.optimization_barrier(jnp.mean(summed, axis=-1, keepdims=True))
    spread = lax.optimization_barrier(jnp.mean(center * center, axis=-1, keepdims=True))
    return center * lax.rsqrt(spread + 1e-05) * gain + shift

def visible(target):
    place = jnp.arange(2 * target, dtype=jnp.int32) % target
    stream = jnp.arange(2 * target, dtype=jnp.int32) // target
    row_place = place[:, None]
    key_place = place[None, :]
    row_stream = stream[:, None]
    key_stream = stream[None, :]
    earlier = (key_stream == 0) & ((row_stream == 0) & (key_place <= row_place) | (row_stream == 1) & (key_place < row_place))
    itself = (key_stream == 1) & (row_stream == 1) & (key_place == row_place)
    return earlier | itself

def attend(query, keys, values, bias, allowed):
    scores = jnp.einsum('qhd,khd->hqk', query, keys, precision=lax.Precision.HIGHEST) * 0.125 + bias
    scores = jnp.where(allowed, low_back(scores), -1e+30)
    weights = jnp.exp(scores - lax.optimization_barrier(jnp.max(scores, axis=-1, keepdims=True)))
    probs = low(weights / lax.optimization_barrier(jnp.sum(weights, axis=-1, keepdims=True)))
    return jnp.einsum('hqk,khd->qhd', probs, values, precision=lax.Precision.HIGHEST)

def layer(params, tokens, encoded, buckets, valid, allowed):
    self_q, self_qb, self_k, self_v, self_vb, self_o, self_ob, bucket_w, bucket_b, cross_q, cross_qb, cross_k, cross_v, cross_vb, cross_o, cross_ob, ffn_in, ffn_inb, ffn_out, ffn_outb, gain_a, shift_a, gain_b, shift_b, gain_c, shift_c = params
    rows = tokens.reshape(2 * TGT, D)
    head_shape = (2 * TGT, HEADS, HEAD_DIM)
    source_shape = (SRC, HEADS, HEAD_DIM)
    query = low_back(low(matmul(rows, self_q) + self_qb)).reshape(head_shape)
    keys = low_back(low(matmul(rows, self_k))).reshape(head_shape)
    values = low_back(low(matmul(rows, self_v) + self_vb)).reshape(head_shape)
    relative = low_back(matmul(rows, bucket_w) + bucket_b).reshape(2 * TGT, HEADS, BUCKETS)
    onehot = (buckets[:, None, :] == jnp.arange(BUCKETS, dtype=jnp.int32)[None, :, None]).astype(jnp.float32)
    bias = jnp.einsum('qbk,qhb->hqk', onehot, relative, precision=lax.Precision.HIGHEST)
    mixed = low_back(low(attend(query, keys, values, bias, allowed).reshape(2 * TGT, D)))
    first = layer_norm(rows + low_back(matmul(mixed, self_o) + self_ob), gain_a, shift_a)
    probe = low_back(low(matmul(low(first), cross_q) + cross_qb)).reshape(head_shape)
    index = low_back(low(matmul(encoded, cross_k))).reshape(source_shape)
    content = low_back(low(matmul(encoded, cross_v) + cross_vb)).reshape(source_shape)
    joined = low_back(low(attend(probe, index, content, 0.0, True).reshape(2 * TGT, D)))
    second = layer_norm(first + low_back(matmul(joined, cross_o) + cross_ob), gain_b, shift_b)
    before = low_back(matmul(low(second), ffn_in) + ffn_inb)
    activity = low(jax.nn.gelu(before, approximate=False))
    third = layer_norm(second + low_back(matmul(activity, ffn_out) + ffn_outb), gain_c, shift_c)
    return (third * valid[:, None]).reshape(2, TGT, D)

def reference(tokens, encoded, cotangent, buckets, lengths, self_q, self_qb, self_k, self_v, self_vb, self_o, self_ob, bucket_w, bucket_b, cross_q, cross_qb, cross_k, cross_v, cross_vb, cross_o, cross_ob, ffn_in, ffn_inb, ffn_out, ffn_outb, gain_a, shift_a, gain_b, shift_b, gain_c, shift_c):
    params = tuple((entry.astype(jnp.float32) for entry in (self_q, self_qb, self_k, self_v, self_vb, self_o, self_ob, bucket_w, bucket_b, cross_q, cross_qb, cross_k, cross_v, cross_vb, cross_o, cross_ob, ffn_in, ffn_inb, ffn_out, ffn_outb, gain_a, shift_a, gain_b, shift_b, gain_c, shift_c)))
    allowed = visible(TGT)

    def one_item(totals, item):
        piece, source, grad_out, bucket, length = item
        valid = jnp.tile((jnp.arange(TGT, dtype=jnp.int32) < length).astype(jnp.float32), 2)

        def local(weights, inputs, memory):
            return layer(weights, inputs, memory, bucket.reshape(2 * TGT, 2 * TGT), valid, allowed)
        result, pull = jax.vjp(local, params, piece.astype(jnp.float32), source.astype(jnp.float32))
        grad_params, grad_piece, grad_source = pull(grad_out.astype(jnp.float32))
        totals = jax.tree.map(jnp.add, totals, grad_params)
        return (totals, (result.astype(jnp.bfloat16), grad_piece, grad_source))
    zeros = tuple((jnp.zeros(entry.shape, jnp.float32) for entry in params))
    totals, (outputs, grad_tokens, grad_encoded) = lax.scan(one_item, zeros, (tokens, encoded, cotangent, buckets, lengths))
    return (outputs, grad_tokens, grad_encoded, totals[0], totals[1], totals[2], totals[3], totals[4], totals[5], totals[6], totals[7], totals[8], totals[9], totals[10], totals[11], totals[12], totals[13], totals[14], totals[15], totals[16], totals[17], totals[18], totals[19], totals[20], totals[21], totals[22], totals[23], totals[24], totals[25])
```

```python
from functools import partial

import jax
import jax.numpy as jnp
from jax import lax
from jax.experimental import pallas as pl
from jax.experimental.pallas import tpu as pltpu
from jax.sharding import PartitionSpec as P

HEAD_DIM = 64
BUCKETS = 32
CORES = 2
ROWS = 32
WIDE = 1024
AHEAD = 3
LINES = 64
LAG = 2
AXES = ("dp", "fsdp")
(
    SELF_Q, SELF_K, SELF_V, BUCKET_W, SELF_O, CROSS_K,
    CROSS_V, CROSS_Q, CROSS_O, FFN_IN, FFN_OUT,
) = MATRICES = tuple(range(11))
(
    SELF_QB, SELF_VB, SELF_OB, CROSS_QB, CROSS_VB, CROSS_OB,
    FFN_OUTB, GAIN_A, SHIFT_A, GAIN_B, SHIFT_B, GAIN_C,
    SHIFT_C, BUCKET_B, FFN_INB,
) = NARROW = tuple(range(11, 26))
VECTORS = NARROW[:13]
WHOLE = (
    SELF_Q, SELF_QB, SELF_K, SELF_V, SELF_VB, SELF_O,
    SELF_OB, BUCKET_W, BUCKET_B, CROSS_Q, CROSS_QB, CROSS_K,
    CROSS_V, CROSS_VB, CROSS_O, CROSS_OB, FFN_IN, FFN_INB,
    FFN_OUT, FFN_OUTB, GAIN_A, SHIFT_A, GAIN_B, SHIFT_B,
    GAIN_C, SHIFT_C,
)
(
    QUERY, KEYS, VALUES, MIXED, FIRST_LOW, PROBE,
    JOINED, SECOND_LOW, INDEX, CONTENT, SUM_FIRST, SUM_SECOND,
    SUM_THIRD, SLOPE, ACTIVITY, SELF_P, CROSS_P, VECTOR,
) = SAVED = tuple(range(18))


RB, EB, CB = 18, 19, 20
SUM_ORDER = (
    FFN_OUT, FFN_IN, CROSS_O, CROSS_Q, CROSS_V, CROSS_K, SELF_O, SELF_V, SELF_K, SELF_Q, BUCKET_W,
)
POOL = 32
ACTIVITIES, SLOPES, COTANGENT, BRANCH_THREE, SECONDS, JOINEDS, PROBES = 0, 4, 8, 9, 13, 17, 18
INDEXES, CONTENTS, FIRSTS = 19, 21, 23
BRANCH_TWO, GRAD_JOINED, GRAD_PROBE, GRAD_INDEX, GRAD_CONTENT, ENCODED = 8, 0, 1, 2, 24, 6
MIXEDS, QUERIES, KEYSES, VALUESES, TOKENS = 9, 10, 17, 18, 19
BRANCH_ONE, GRAD_MIXED, GRAD_QUERY, GRAD_KEYS, GRAD_VALUES, GRAD_RELATIVE = 20, 21, 22, 0, 8, 23
PARTIALS, PARTIAL_OTHER, PARTIAL_DIAGONAL, PARTIAL_NEXT = 25, 29, 30, 31
GATHER_ORDER = (
    SELF_Q, SELF_K, SELF_V, BUCKET_W, SELF_O, CROSS_Q, CROSS_K, CROSS_V,
    FFN_IN, FFN_IN, CROSS_O, FFN_IN, FFN_IN, FFN_OUT, FFN_OUT, FFN_OUT, FFN_OUT,
)
GROUP = 4
NEXT, OTHER, DIAGONAL = 1, 2, 3


def chips(dp, fsdp):
    square = fsdp
    return (dp // (CORES * square), square, CORES, fsdp)


def place(sizes):
    far, near, cores, side = sizes
    row = lax.axis_index(AXES[0])
    return (row // (near * cores), lax.rem(row // cores, near), lax.rem(row, cores), lax.axis_index(AXES[1]))


def device_at(sizes, spot):
    z, y, c, x = spot
    return ((z * sizes[1] + y) * sizes[2] + c, x)


def moved(spot, level, digit):
    return spot[:level] + (digit,) + spot[level + 1 :]


def peer_at(sizes, me, level, step):
    if level < GROUP:
        return moved(me, level, lax.rem(me[level] + step, sizes[level]))
    core = lax.rem(me[2] + step // sizes[3], sizes[2])
    return (me[0], me[1], core, lax.rem(me[3] + step % sizes[3], sizes[3]))


def reach(sizes, level):
    return sizes[level] if level < GROUP else sizes[2] * sizes[3]


def number_in_group(sizes, spot):
    return spot[2] * sizes[3] + spot[3]


def enter(sizes, me):
    barrier = pltpu.get_barrier_semaphore()
    peers = [(level, step) for level in range(GROUP) for step in range(1, sizes[level])]
    peers += [
        (GROUP, step) for step in range(sizes[3] + 1, sizes[2] * sizes[3]) if step % sizes[3]
    ]
    for level, step in peers:
        pl.semaphore_signal(
            barrier,
            inc=1,
            device_id=device_at(sizes, peer_at(sizes, me, level, step)),
            device_id_type=pl.DeviceIdType.MESH,
        )
    pl.semaphore_wait(barrier, len(peers))


ROUTES = ((0, 1, 3, 2), (0, 3, 1, 2), (3, 1, 0, 2))


def levels_of(which):
    return (0, 1) if which == FFN_OUT else (0, 1, 2, 3)


def gather_route(which, route):
    if which == FFN_OUT:
        return (0, 1)
    return (GROUP, 0, 1) if which == FFN_IN else ROUTES[route]


def sum_route(which, route):
    if which == FFN_OUT:
        return (1, 0)
    return (1, 0, GROUP) if which == FFN_IN else (2,) + ROUTES[route][2::-1]


def without(levels, done):
    gone = tuple(done) + ((2, 3) if GROUP in done else ())
    return tuple(level for level in levels if level not in gone)


def units_of(which, rows, columns):
    if which in (-1, FFN_IN, FFN_OUT) or columns % 256:
        return [(0, rows, 0, columns, 0)]
    half = columns // 2
    return [(0, rows, 0, half, 0), (0, rows, half, half, 1)]


def slots(sizes):
    first = []
    total = 0
    for level in range(GROUP + 1):
        first.append(total)
        total += reach(sizes, level) - 1
    return first, total


def parts_of(devices, which, shape):
    rows, columns = shape[-2:]
    wide = min(columns, WIDE * ROWS // rows)
    if which == FFN_IN:
        wide = WIDE // GROUP
    return (rows, wide), columns // wide


def lane_tile(step, wide):
    if isinstance(step, int):
        return pl.ds(step * wide, wide)
    return pl.ds(pl.multiple_of(step * wide, wide), wide)


def tiles(count, body):
    for step in range(count):
        body(step, 0)


def normal(summed, gain, shift):
    center = summed - jnp.mean(summed, axis=-1, keepdims=True)
    spread = jnp.mean(center * center, axis=-1, keepdims=True)
    return center * lax.rsqrt(spread + 1e-05) * gain + shift


def softmax_rows(scores):
    weights = jnp.exp(scores - jnp.max(scores, axis=-1, keepdims=True))
    return weights * (1.0 / jnp.sum(weights, axis=-1, keepdims=True))


def forward_kernel(sizes, chunks, saved, *refs):
    far, near, cores, side = sizes
    devices = far * near * cores * side
    count = len(MATRICES)
    rows, enc, buckets, valid, small = refs[:5]
    shards, refs = refs[5 : 5 + count], refs[5 + count :]
    outputs, refs = refs[0], refs[1:]
    whole, refs = refs[:count], refs[count:]
    kept, refs = refs[: len(saved)], refs[len(saved) :]
    held = dict(zip(saved, refs[: len(saved)]))
    refs = refs[len(saved) :]
    here, refs = refs[:count], refs[count:]
    vectors, relative, hidden, first, second, wide_bias, partial_out, partial_in, room = refs[:9]
    kept_sem, whole_sem, pair_send, pair_recv, own_sem, send_sem, recv_sem = refs[9:]
    vector = held[VECTOR]
    me = place(sizes)
    slot_of, unused = slots(sizes)
    total = len(chunks)
    units = []
    units_in = []
    for number, (which, part, tall, wide) in enumerate(chunks):
        block_rows = small.shape[0] if which < 0 else whole[which].shape[-2]
        own_units = [(number,) + unit for unit in units_of(which, block_rows, wide)]
        units_in.append(range(len(units), len(units) + len(own_units)))
        units += own_units

    def region(unit, spot, done):
        number, row, tall_rows, column, columns, route = units[unit]
        which, part, tall, wide = chunks[number]
        stay = without(levels_of(which), done)
        index = tuple(
            spot[level] if level in stay else slice(None) for level in levels_of(which)
        )
        if which < 0:
            return vectors.at[index]
        return here[which].at[(part,) + index + (pl.ds(row, tall_rows), pl.ds(column, columns))]

    def own(unit, spot):
        number, row, tall_rows, column, columns, route = units[unit]
        which, part, tall, wide = chunks[number]
        if which < 0:
            return small
        shard = shards[which]
        if which == FFN_IN:
            shard = shard.at[number_in_group(sizes, spot)]
        return shard.at[pl.ds(row, tall_rows), pl.ds(part * wide + column, columns)]

    def route_of(unit):
        return gather_route(chunks[units[unit][0]][0], units[unit][-1])

    def copy(unit, stage, step, from_peer):
        order = route_of(unit)
        level = order[stage]
        size = reach(sizes, level)
        done = order[:stage]
        slot = slot_of[level] + step - 1
        if from_peer:
            peer = peer_at(sizes, me, level, step if level == GROUP else size - step)
            target = region(unit, peer, done)
            source = target
        else:
            peer = peer_at(sizes, me, level, step)
            target = region(unit, me, done)
            source = own(unit, peer) if level == GROUP else target
        return pltpu.make_async_remote_copy(
            src_ref=source,
            dst_ref=target,
            send_sem=send_sem.at[unit, slot],
            recv_sem=recv_sem.at[unit, slot],
            device_id=device_at(sizes, peer),
            device_id_type=pl.DeviceIdType.MESH,
        )

    def steps(unit, stage):
        order = route_of(unit)
        return range(1, reach(sizes, order[stage])) if stage < len(order) else ()

    def keep(unit):
        return pltpu.make_async_copy(own(unit, me), region(unit, me, ()), own_sem.at[unit])

    def start(number, stage):
        for unit in units_in[number]:
            if stage == 0:
                keep(unit).wait()
            for step in steps(unit, stage):
                copy(unit, stage, step, False).start()

    def pass_on(number, stage):
        for unit in units_in[number]:
            for step in steps(unit, stage):
                copy(unit, stage, step, True).wait_recv()
            if stage < 3:
                for step in steps(unit, stage + 1):
                    copy(unit, stage + 1, step, False).start()

    def turn(now):
        if now + AHEAD < total:
            start(now + AHEAD, 0)
        for stage in range(4):
            number = now - LAG * stage
            if 0 <= number < total:
                pass_on(number, stage)

    def write(number):
        which, part, tall, wide = chunks[number]
        return pltpu.make_async_copy(
            here[which].at[part], whole[which].at[part], whole_sem.at[number]
        )

    def weight(number, step=None, tile=256):
        which, part, tall, wide = chunks[number]
        if step is None:
            return here[which][part].reshape(-1, wide)
        return here[which][part, :, :, :, :, :, lane_tile(step, tile)].reshape(-1, tile)

    def row_of(name):
        return NARROW.index(name)

    def project(number, left, into, bias=None, plus=None):
        wide = chunks[number][3]

        def body(step, carry):
            columns = lane_tile(step, 256)
            result = product(left[...], weight(number, step))
            if bias is not None:
                result = result + vector[pl.ds(row_of(bias), 1), columns]
            if plus is not None:
                result = result + plus[:, columns].astype(jnp.float32)
            into[:, columns] = result.astype(into.dtype)
            return carry

        tiles(wide // 256, body)

    def save(*names):
        for name in names:
            number = saved.index(name)
            pltpu.make_async_copy(held[name], kept[number], kept_sem.at[number]).start()

    def norm(summed, gain, shift, into, low):
        def body(step, carry):
            lines = pl.ds(pl.multiple_of(step * 64, 64), 64)
            result = normal(
                summed[lines, :],
                vector[pl.ds(row_of(gain), 1), :],
                vector[pl.ds(row_of(shift), 1), :],
            )
            if into is not None:
                into[lines, :] = result
                low[lines, :] = result.astype(low.dtype)
            else:
                low[lines, :] = (result * valid[lines, :]).astype(low.dtype)
            return carry

        lax.fori_loop(0, summed.shape[0] // 64, body, 0)

    def unpack():
        spots = []
        for index in range(devices):
            x = index % side
            c = index // side % cores
            y = index // (side * cores) % near
            spots.append((index // (side * cores * near), y, c, x))
        blocks = [vectors[spot].astype(jnp.float32) for spot in spots]

        def joined(number, fits):
            return sum(blocks[number * fits + 1 : (number + 1) * fits], blocks[number * fits])

        fits = devices * 128 // vector.shape[1]
        for number in range(devices // fits):
            vector[:, pl.ds(128 * number, 128)] = joined(number, fits)
        row = row_of(BUCKET_B)
        fits = devices * 128 // relative.shape[1]
        for number in range(devices // fits):
            vector[pl.ds(row, 1), pl.ds(128 * number, 128)] = joined(number, fits)[row : row + 1]
        row = row_of(FFN_INB)
        for number in range(far * near):
            spot = (number // near, number % near, me[2], me[3])
            wide_bias[:, pl.ds(128 * number, 128)] = vectors[spot].astype(jnp.float32)[row : row + 1]
        hidden[...] = jnp.where(visible(hidden.shape[0] // 2), 0.0, -1e30)

    def heads(low, high, query, keys, values, probs, mixed, biased):
        lane = lax.broadcasted_iota(jnp.int32, (1, 2 * HEAD_DIM), 1)

        def body(pair, carry):
            columns = lane_tile(pair, 2 * HEAD_DIM)
            one, key, value = query[:, columns], keys[:, columns], values[:, columns]
            reach = keys.shape[0]
            for half in range(2):
                mine = lane // HEAD_DIM == half
                room[half, :, pl.ds(0, reach)] = product_right(
                    jnp.where(mine, one, 0).astype(one.dtype), key
                )
            for half in range(2):
                for line in range(0, one.shape[0], LINES):
                    lines = pl.ds(line, LINES)
                    scores = room[half, lines, pl.ds(0, reach)] * 0.125
                    if biased:
                        fit = 128 // BUCKETS
                        table = relative[lines, lane_tile(pair * 2 // fit, 128)]
                        offset = lax.rem(pair * 2, fit) * BUCKETS + half * BUCKETS
                        found = [
                            jnp.take_along_axis(
                                table, buckets[lines, pl.ds(at, 128)] + offset, axis=1
                            )
                            for at in range(0, reach, 128)
                        ]
                        scores = scores + jnp.concatenate(found, axis=1) + hidden[lines, :]
                    probs[pair, lines, pl.ds(half * reach, reach)] = softmax_rows(scores).astype(
                        jnp.bfloat16
                    )
            results = [
                product(probs[pair, :, pl.ds(half * reach, reach)], value) for half in range(2)
            ]
            mixed[:, columns] = jnp.where(lane < HEAD_DIM, *results).astype(mixed.dtype)
            return carry

        lax.fori_loop(low, high, body, 0)

    def self_heads(low, high):
        heads(
            low, high, held[QUERY], held[KEYS], held[VALUES], held[SELF_P], held[MIXED], True
        )

    def cross_heads(low, high):
        heads(
            low, high, held[PROBE], held[INDEX], held[CONTENT], held[CROSS_P], held[JOINED], False
        )

    def to_item(item, source, target, number):
        return pltpu.make_async_remote_copy(
            src_ref=source,
            dst_ref=target,
            send_sem=pair_send.at[number],
            recv_sem=pair_recv.at[number],
            device_id=device_at(sizes, peer_at(sizes, me, GROUP, item)),
            device_id_type=pl.DeviceIdType.MESH,
        )

    lows = held[SECOND_LOW]

    def share(item):
        if item == DIAGONAL:
            return to_item(OTHER, lows.at[NEXT], lows.at[DIAGONAL], DIAGONAL)
        return to_item(item, lows.at[0], lows.at[item], item)

    def partial(kind, part):
        return to_item(
            NEXT if kind == 2 else OTHER,
            partial_out.at[kind, part],
            partial_in.at[kind, part],
            GROUP + 3 * part + kind,
        )

    amount, width = rows.shape
    def feed(number, item):
        part, tall, wide = chunks[number][1:]
        columns = pl.ds(part * wide, wide)
        room[0, :, pl.ds(0, wide)] = product(lows[item], weight(number))

        def body(step, carry):
            for line in range(2):
                lines = pl.ds(pl.multiple_of(step * 64 + line * 32, 32), 32)
                before = room[0, lines, pl.ds(0, wide)] + wide_bias[:, columns]
                error = 1.0 + lax.erf(before * (0.5**0.5))
                held[ACTIVITY][item, lines, columns] = (0.5 * before * error).astype(jnp.bfloat16)
                slope = 0.5 * error + before * jnp.exp(-0.5 * before * before) * (
                    0.3989422804014327
                )
                held[SLOPE][item, lines, columns] = slope.astype(jnp.bfloat16)
            return carry

        lax.fori_loop(0, amount // 64, body, 0)

    def back(number):
        part, tall, wide = chunks[number][1:]
        columns = pl.ds(part * wide, wide)
        activity = held[ACTIVITY]
        partial_out[0, part] = product(activity[OTHER], weight(number)).astype(jnp.bfloat16)
        partial(0, part).start()
        partial_out[1, part] = product(activity[DIAGONAL], weight(number)).astype(jnp.bfloat16)
        partial(1, part).start()
        first[:, columns] = product(activity[NEXT], weight(number))
        held[SUM_THIRD][:, columns] = (
            product(activity[0], weight(number))
            + vector[pl.ds(row_of(FFN_OUTB), 1), columns]
            + second[:, columns]
        )

    def relay(part):
        wide = width // GROUP
        partial(1, part).wait_recv()
        total_of = first[:, pl.ds(part * wide, wide)] + partial_in[1, part].astype(jnp.float32)
        partial_out[2, part] = total_of.astype(jnp.bfloat16)
        partial(2, part).start()

    pairs = held[QUERY].shape[1] // (2 * HEAD_DIM)

    def compute(number):
        which, part, tall, wide = chunks[number]
        if which < 0:
            unpack()
            save(VECTOR)
            return
        write(number).start()
        name = MATRICES[which]
        if name == SELF_Q:
            project(number, rows, held[QUERY], SELF_QB)
            save(QUERY)
        elif name == SELF_K:
            project(number, rows, held[KEYS])
            save(KEYS)
        elif name == SELF_V:
            project(number, rows, held[VALUES], SELF_VB)
            save(VALUES)
        elif name == BUCKET_W:
            project(number, rows, relative, BUCKET_B)
            self_heads(0, pairs // 2)
        elif name == SELF_O:
            self_heads(pairs // 2, pairs)
            save(SELF_P, MIXED)
            project(number, held[MIXED], held[SUM_FIRST], SELF_OB, rows)
            save(SUM_FIRST)
            norm(held[SUM_FIRST], GAIN_A, SHIFT_A, first, held[FIRST_LOW])
            save(FIRST_LOW)
        elif name == CROSS_K:
            project(number, enc, held[INDEX])
            save(INDEX)
        elif name == CROSS_V:
            project(number, enc, held[CONTENT], CROSS_VB)
            save(CONTENT)
            cross_heads(0, pairs // 2)
        elif name == CROSS_Q:
            project(number, held[FIRST_LOW], held[PROBE], CROSS_QB)
            save(PROBE)
        elif name == CROSS_O:
            cross_heads(pairs // 2, pairs)
            save(CROSS_P, JOINED)
            project(number, held[JOINED], held[SUM_SECOND], CROSS_OB, first)
            save(SUM_SECOND)
            norm(held[SUM_SECOND], GAIN_B, SHIFT_B, second, lows.at[0])
            share(NEXT).start()
            share(OTHER).start()
            feed(number - 2, 0)
            feed(number - 1, 0)
        elif name == FFN_IN and part >= 2:
            feed(number, 0)
            if part == 2:
                share(OTHER).wait_recv()
                for earlier in (number - 3, number - 2):
                    feed(earlier, OTHER)
                share(NEXT).wait_recv()
                share(DIAGONAL).start()
                for earlier in (number - 3, number - 2):
                    feed(earlier, NEXT)
                share(DIAGONAL).wait_recv()
                for earlier in (number - 3, number - 2):
                    feed(earlier, DIAGONAL)
                save(SECOND_LOW)
            for item in (OTHER, NEXT, DIAGONAL):
                feed(number, item)
            if part == 3:
                save(SLOPE, ACTIVITY)
        elif name == FFN_OUT:
            back(number)
            if part > 0:
                relay(part - 1)

    for unit in range(len(units)):
        keep(unit).start()
    enter(sizes, me)
    for number in range(min(AHEAD, total)):
        start(number, 0)
    for now in range(total + 3 * LAG):
        turn(now)
        if now >= 3 * LAG:
            compute(now - 3 * LAG)
    relay(GROUP - 1)
    wide = width // GROUP
    for part in range(GROUP):
        partial(0, part).wait_recv()
        partial(2, part).wait_recv()
        held[SUM_THIRD][:, pl.ds(part * wide, wide)] += partial_in[0, part].astype(
            jnp.float32
        ) + partial_in[2, part].astype(jnp.float32)
    save(SUM_THIRD)
    norm(held[SUM_THIRD], GAIN_C, SHIFT_C, None, outputs)
    for unit in range(len(units)):
        for stage in range(4):
            for step in steps(unit, stage):
                copy(unit, stage, step, False).wait_send()
    for item in (NEXT, OTHER, DIAGONAL):
        share(item).wait_send()
    for part in range(GROUP):
        for kind in range(3):
            partial(kind, part).wait_send()
    for number in range(1, total):
        write(number).wait()
    for number, name in enumerate(saved):
        pltpu.make_async_copy(held[name], kept[number], kept_sem.at[number]).wait()


def forward_all(sizes, small, blocks, rows, enc, buckets, valid):
    devices = sizes[0] * sizes[1] * sizes[2] * sizes[3]
    chunks = [(-1, 0, False, 128)]
    shapes = []
    units = 1
    for which, block in enumerate(blocks):
        part, parts = parts_of(devices, which, block.shape)
        shape = tuple(sizes[level] for level in levels_of(which))
        shapes.append(jax.ShapeDtypeStruct((parts,) + shape + part, block.dtype))
    done = dict.fromkeys(MATRICES, 0)
    for which in GATHER_ORDER:
        part = shapes[which].shape[-2:]
        units += len(units_of(which, *part))
        chunks.append((which, done[which], part[0] > ROWS, part[1]))
        done[which] += 1
    amount, width = rows.shape
    source = enc.shape[0]
    hidden_units = blocks[MATRICES.index(FFN_IN)].shape[-1]
    buckets_wide = blocks[MATRICES.index(BUCKET_W)].shape[1]
    head_count = width // HEAD_DIM
    low, full = jnp.bfloat16, jnp.float32
    one, two = (amount, width), (source, width)
    saved = {
        QUERY: (one, low), KEYS: (one, low), VALUES: (one, low), MIXED: (one, low),
        FIRST_LOW: (one, low), PROBE: (one, low), JOINED: (one, low),
        SECOND_LOW: ((GROUP,) + one, low), INDEX: (two, low), CONTENT: (two, low),
        SUM_FIRST: (one, full), SUM_SECOND: (one, full), SUM_THIRD: (one, full),
        SLOPE: ((GROUP, amount, hidden_units), low), ACTIVITY: ((GROUP, amount, hidden_units), low),
        SELF_P: ((head_count // 2, amount, 2 * amount), low),
        CROSS_P: ((head_count // 2, amount, 2 * source), low),
        VECTOR: ((16, width), full),
    }
    names = SAVED
    unused, places = slots(sizes)
    any_spec = pl.BlockSpec(memory_space=pl.ANY)
    vmem_spec = pl.BlockSpec(memory_space=pltpu.VMEM)
    held = [pltpu.VMEM(*saved[name]) for name in names]
    results = pl.pallas_call(
        partial(forward_kernel, sizes, chunks, names),
        out_shape=[jax.ShapeDtypeStruct(one, low)]
        + shapes
        + [jax.ShapeDtypeStruct(*saved[name]) for name in names],
        in_specs=[vmem_spec] * 4 + [any_spec] * (1 + len(blocks)),
        out_specs=[vmem_spec] + [any_spec] * (len(shapes) + len(names)),
        scratch_shapes=held
        + [pltpu.VMEM(entry.shape, entry.dtype) for entry in shapes]
        + [
            pltpu.VMEM(sizes + small.shape, low),
            pltpu.VMEM((amount, buckets_wide), full),
            pltpu.VMEM((amount, amount), full),
            pltpu.VMEM(one, full),
            pltpu.VMEM(one, full),
            pltpu.VMEM((1, hidden_units), full),
            pltpu.VMEM((3, GROUP, amount, width // GROUP), low),
            pltpu.VMEM((3, GROUP, amount, width // GROUP), low),
            pltpu.VMEM((2, amount, max(amount, source)), full),
            pltpu.SemaphoreType.DMA((len(names),)),
            pltpu.SemaphoreType.DMA((len(chunks),)),
            pltpu.SemaphoreType.DMA((4 * GROUP,)),
            pltpu.SemaphoreType.DMA((4 * GROUP,)),
            pltpu.SemaphoreType.DMA((units,)),
            pltpu.SemaphoreType.DMA((units, places)),
            pltpu.SemaphoreType.DMA((units, places)),
        ],
        compiler_params=pltpu.CompilerParams(
            collective_id=0, has_side_effects=True, vmem_limit_bytes=63 * 1024 * 1024
        ),
        cost_estimate=pl.CostEstimate(flops=10**10, bytes_accessed=1 << 27, transcendentals=10**7),
        name="forward_all",
    )(rows, enc, buckets, valid, small, *blocks)
    whole = dict(zip(MATRICES, results[1 : 1 + len(blocks)]))
    return results[0], whole, dict(zip(names, results[1 + len(blocks) :]))


def backward_kernel(sizes, chunks, flat_room, *refs):
    far, near, cores, side = sizes
    devices = far * near * cores * side
    count = len(MATRICES)
    cotangent, buckets, valid, rows_in, enc_in = refs[:5]
    kept, refs = refs[5 : 5 + len(SAVED)], refs[5 + len(SAVED) :]
    whole, refs = refs[:count], refs[count:]
    small_out, shares, refs = refs[0], refs[1 : 1 + count], refs[1 + count :]
    tokens_out, encoded_out, refs = refs[0], refs[1], refs[2:]
    pool, full, acc, vector, sums, wide_sums, small, relative, picked, room, steep = refs[:11]
    low_slot, tall_slot, self_probs, cross_probs, flat_ring, tall_ring, flat_in = refs[11:18]
    refs = refs[18:]
    total = len(chunks) + 1
    units = []
    units_in = []
    inbox = []
    flats = []
    for number in range(total):
        if number < total - 1:
            which, tall_rows, tall, wide, column = chunks[number]
            own_units = units_of(which, tall_rows, wide)
            if which not in (FFN_IN, FFN_OUT):
                flats.append(number)
        else:
            which = -1
            own_units = units_of(which, *small.shape[4:])
        units_in.append(range(len(units), len(units) + len(own_units)))
        for unit in own_units:
            units.append((number,) + unit)
            if flats and flats[-1] == number:
                shelf = flat_in.at[pl.ds((len(flats) - 1) % flat_room, 1)]
                shelf = shelf.at[:, :, :, :, :, pl.ds(unit[2], unit[3])]
                inbox.append((shelf,) + tuple(refs[:3]))
                refs = refs[3:]
            else:
                deep = len(sum_route(which, 0))
                inbox.append(tuple(refs[:deep]))
                refs = refs[deep:]
    load_sem, slot_sem, self_sem, cross_sem, out_sem, credit = refs[:6]
    pair_send, pair_recv, send_sem, recv_sem = refs[6:]
    me = place(sizes)
    first, unused = slots(sizes)
    z, y, c, x = me
    amount, width = rows_in.shape
    source = enc_in.shape[0]
    pairs = width // (2 * HEAD_DIM)
    slab = width // far

    def loading(which, number, height=1):
        array = {RB: rows_in, EB: enc_in, CB: cotangent}.get(which)
        array = kept[which] if array is None else array
        if which in (SUM_FIRST, SUM_SECOND, SUM_THIRD):
            return [(array, full.at[number], which)]
        if which == VECTOR:
            return [(array, vector, which)]
        if height == 1:
            return [(array, pool.at[number], which)]
        if len(array.shape) == 3:
            return [
                (
                    array.at[part],
                    pool.at[number + part],
                    which,
                )
                for part in range(height)
            ]
        return [
            (array.at[pl.ds(part * amount, amount)], pool.at[number + part], which)
            for part in range(height)
        ]

    semaphores = {}
    waiting = {}

    def fetch(which, number, height=1):
        waiting[which] = []
        for source_ref, target, unused_name in loading(which, number, height):
            semaphores[which, len(waiting[which])] = len(semaphores)
            one = pltpu.make_async_copy(source_ref, target, load_sem.at[len(semaphores) - 1])
            one.start()
            waiting[which].append(one)

    def ready(*names):
        for which in names:
            for one in waiting.pop(which):
                one.wait()

    order = [FFN_IN, CROSS_O, CROSS_Q, SELF_O, CROSS_K, CROSS_V, SELF_Q, SELF_K, SELF_V, BUCKET_W]

    def weight_copies(number):
        which = order[number]
        parts, wide = whole[which].shape[0], whole[which].shape[-1]
        return [
            pltpu.make_async_copy(
                whole[which].at[part],
                low_slot.at[number % 2, :, :, :, :, :, pl.ds(part * wide, wide)],
                slot_sem.at[number % 2 * GROUP + part],
            )
            for part in range(parts)
        ]

    def weight_fetch(number):
        if number < len(order):
            for one in weight_copies(number):
                one.start()

    def weight_ready(number):
        for one in weight_copies(number):
            one.wait()

    def tall_copy():
        return pltpu.make_async_copy(whole[FFN_OUT], tall_slot, slot_sem.at[2 * GROUP])

    def row_of(name):
        return NARROW.index(name)

    def through(which, left, into, fresh=False):
        number = order.index(which)
        wide = whole[which].shape[0] * whole[which].shape[-1]

        def body(step, carry):
            columns = lane_tile(step, slab)
            piece = low_slot[number % 2, step, :, :, :, :, pl.ds(0, wide)].reshape(slab, wide)
            result = product_right(left(), piece)
            if fresh:
                into[:, columns] = result.astype(into.dtype)
            else:
                into[:, columns] += result
            return carry

        tiles(far, body)

    def back_through(which, left, into, fresh=False):
        weight_ready(order.index(which))
        through(which, left, into, fresh)
        weight_fetch(order.index(which) + 2)

    def norm_backward(summed, gain, shift, bias, low, first_grad):
        def body(step, carry):
            lines = pl.ds(pl.multiple_of(step * 64, 64), 64)
            center = summed[lines, :]
            center = center - jnp.mean(center, axis=-1, keepdims=True)
            scale = lax.rsqrt(jnp.mean(center * center, axis=-1, keepdims=True) + 1e-05)
            unit = center * scale
            if first_grad is not None:
                grad = first_grad[lines, :].astype(jnp.float32) * valid[lines, :]
            else:
                grad = acc[lines, :]
            inner = grad * vector[pl.ds(row_of(gain), 1), :]
            inner = inner - jnp.mean(inner, axis=-1, keepdims=True) - unit * jnp.mean(
                inner * unit, axis=-1, keepdims=True
            )
            inner = inner * scale
            branch = inner.astype(jnp.bfloat16)
            acc[lines, :] = inner
            low[lines, :] = branch
            sums[pl.ds(row_of(gain), 1), :] += jnp.sum(grad * unit, axis=0, keepdims=True)
            sums[pl.ds(row_of(shift), 1), :] += jnp.sum(grad, axis=0, keepdims=True)
            sums[pl.ds(row_of(bias), 1), :] += jnp.sum(
                branch.astype(jnp.float32), axis=0, keepdims=True
            )
            return carry

        lax.fori_loop(0, amount // 64, body, 0)

    def feed_backward(item):
        parts, wide = whole[FFN_OUT].shape[0], whole[FFN_OUT].shape[-1]
        tile = near * chunks[0][1]

        def body(step, carry):
            columns = lane_tile(step, tile)
            grad = 0.0
            for part in range(parts):
                piece = tall_slot[part, step].reshape(tile, wide)
                left = pool[BRANCH_THREE + item, :, pl.ds(part * wide, wide)]
                grad = grad + product_right(left, piece)
            slope = pool[SLOPES + item, :, columns].astype(jnp.float32)
            grad = (grad * slope).astype(jnp.bfloat16)
            pool[SLOPES + item, :, columns] = grad
            wide_sums[:, columns] += jnp.sum(grad.astype(jnp.float32), axis=0, keepdims=True)
            return carry

        tiles(far, body)

    def probs_copy(which, pair, slot):
        buffer, sem = (cross_probs, cross_sem) if which == CROSS_P else (self_probs, self_sem)
        return pltpu.make_async_copy(kept[which].at[pair], buffer.at[slot], sem.at[slot])

    def heads_backward(which, low, high, places, tall):
        query, keys, values, grad_out, to_query, to_keys, to_values = places
        buffer = cross_probs if which == CROSS_P else self_probs
        lane = lax.broadcasted_iota(jnp.int32, (1, 2 * HEAD_DIM), 1)
        span = tall * amount

        def body(pair, carry):
            columns = lane_tile(pair, 2 * HEAD_DIM)
            slot = lax.rem(pair, 2)
            probs_copy(which, pair, slot).wait()

            @pl.when(pair + 1 < pairs)
            def _():
                probs_copy(which, pair + 1, 1 - slot).start()

            one = pool[query, :, columns]
            grad = pool[grad_out, :, columns]
            key = pool[pl.ds(keys, tall), :, columns].reshape(span, 2 * HEAD_DIM)
            value = pool[pl.ds(values, tall), :, columns].reshape(span, 2 * HEAD_DIM)
            found = []
            for half in range(2):
                mine = lane // HEAD_DIM == half
                room[half, :, pl.ds(0, span)] = product_right(
                    jnp.where(mine, grad, 0).astype(grad.dtype), value
                )
            for half in range(2):
                for line in range(0, amount, LINES):
                    lines = pl.ds(line, LINES)
                    prob = buffer[slot, lines, pl.ds(half * span, span)].astype(jnp.float32)
                    weighted = prob * room[half, lines, pl.ds(0, span)]
                    scores = weighted - prob * jnp.sum(weighted, axis=-1, keepdims=True)
                    scores = scores.astype(jnp.bfloat16)
                    steep[half, lines, pl.ds(0, span)] = scores
                    if which == SELF_P:
                        picked[half, lines, :] = scores[:, :target].astype(jnp.float32)
                if which == SELF_P:
                    gather_buckets(pair, half)
            for half in range(2):
                scores = steep[half, :, pl.ds(0, span)]
                prob = buffer[slot, :, pl.ds(half * span, span)]
                found.append(
                    (
                        product(scores, key) * 0.125,
                        product_left(scores, one) * 0.125,
                        product_left(prob, grad),
                    )
                )
            if which == SELF_P:
                spread_buckets(pair)
            merged = [
                jnp.where(lane < HEAD_DIM, left, right).astype(jnp.bfloat16)
                for left, right in zip(*found)
            ]
            pool[to_query, :, columns] = merged[0]
            pool[pl.ds(to_keys, tall), :, columns] = merged[1].reshape(tall, amount, 2 * HEAD_DIM)
            pool[pl.ds(to_values, tall), :, columns] = merged[2].reshape(tall, amount, 2 * HEAD_DIM)
            biases = (SELF_QB, SELF_VB) if which == SELF_P else (CROSS_QB, CROSS_VB)
            for bias, grads in zip(biases, (merged[0], merged[2])):
                sums[pl.ds(row_of(bias), 1), columns] = jnp.sum(
                    grads.astype(jnp.float32), axis=0, keepdims=True
                )
            return carry

        lax.fori_loop(low, high, body, 0)

    target = amount // 2
    fit = 128 // BUCKETS

    def gather_buckets(pair, half):
        own = steep[half, pl.ds(target, target), pl.ds(target, target)].astype(jnp.float32)
        own = jnp.sum(own, axis=1, keepdims=True)
        line = lax.broadcasted_iota(jnp.int32, (target, target), 0)
        lane = lax.broadcasted_iota(jnp.int32, (target, target), 1)
        bucket = jnp.sum(
            jnp.where(line == lane, buckets[target:, target:], 0).astype(jnp.float32),
            axis=1,
            keepdims=True,
        ).astype(jnp.int32)
        offset = lax.rem(pair * 2, fit) * BUCKETS + half * BUCKETS
        block = lane_tile(pair * 2 // fit, 128)
        relative[pl.ds(target, target), block] += jnp.where(lane == bucket + offset, own, 0.0)

    def spread_buckets(pair):
        block = lane_tile(pair * 2 // fit, 128)
        some = 8
        line = lax.broadcasted_iota(jnp.int32, (some * target, 128), 0)
        lane = lax.broadcasted_iota(jnp.int32, (some * target, 128), 1)

        def body(step, carry):
            for half in range(2):
                offset = lax.rem(pair * 2, fit) * BUCKETS + half * BUCKETS
                held = [
                    jnp.where(
                        buckets[:, :target] == some * step + other, picked[half], 0.0
                    ).astype(jnp.bfloat16)
                    for other in range(some)
                ]
                chosen = lane == offset + some * step + line // target
                relative[:, block] += product(
                    jnp.concatenate(held, axis=1), jnp.where(chosen, 1.0, 0.0).astype(jnp.bfloat16)
                )
            return carry

        lax.fori_loop(0, BUCKETS // some, body, 0)

    def held(number):
        if number == total - 1:
            return small, None
        tall, wide = chunks[number][2:4]
        same = [other for other in range(number) if chunks[other][2] == tall]
        ring = tall_ring if tall else flat_ring
        size = ring.shape[0]
        ref = ring.at[len(same) % size]
        if not tall:
            ref = ref.at[:, :, :, :, :, pl.ds(0, wide)]
        return ref, same[-size] if len(same) >= size else None

    def stage_of(unit, stage):
        number, row, tall_rows, column, columns, route = units[unit]
        which = chunks[number][0] if number < total - 1 else -1
        order_of = sum_route(which, route)
        before = without(levels_of(which), order_of[:stage])
        if stage == 0:
            from_ref = held(number)[0]
            if number < total - 1:
                every = (slice(None),) * len(levels_of(which))
                from_ref = from_ref.at[every + (pl.ds(row, tall_rows), pl.ds(column, columns))]
        else:
            from_ref = inbox[unit][stage - 1].at[0]
        return from_ref, before, order_of[stage], inbox[unit][stage]

    def pick(ref, levels, level, spot, step=None):
        index = []
        for other in levels:
            if other == level or (level == GROUP and other in (2, 3)):
                index.append(spot[other])
            elif other == 0 and step is not None:
                index.append(step)
            else:
                index.append(slice(None))
        return ref.at[tuple(index)] if index else ref

    def stages(unit):
        number = units[unit][0]
        return len(sum_route(chunks[number][0] if number < total - 1 else -1, 0))

    def copies(unit, stage):
        if stage >= stages(unit):
            return []
        from_ref, before, level, into = stage_of(unit, stage)
        found = []
        for step in range(1, reach(sizes, level)):
            peer = peer_at(sizes, me, level, step)
            slot = first[level] + step - 1
            found.append(
                pltpu.make_async_remote_copy(
                    src_ref=pick(from_ref, before, level, peer),
                    dst_ref=into.at[step - 1],
                    send_sem=send_sem.at[unit, slot],
                    recv_sem=recv_sem.at[unit, slot],
                    device_id=device_at(sizes, peer),
                    device_id_type=pl.DeviceIdType.MESH,
                )
            )
        return found

    def start(number):
        if number in flats and flats.index(number) >= flat_room:
            pl.semaphore_wait(credit, cores - 1)
        for unit in units_in[number]:
            for one in copies(unit, 0):
                one.start()

    waited = set()

    def sent(number, stage):
        for unit in units_in[number]:
            if (unit, stage) not in waited:
                waited.add((unit, stage))
                for one in copies(unit, stage):
                    one.wait_send()

    def add(unit, stage):
        if stage >= stages(unit):
            return
        from_ref, before, level, into = stage_of(unit, stage)
        after = without(before, (level,))
        number, row, tall_rows, column, columns, route = units[unit]
        last = stage == stages(unit) - 1
        if last and number < total - 1 and chunks[number][0] == FFN_IN:
            spot = (pl.ds(row, tall_rows), pl.ds(chunks[number][4] + column, columns))
            shares[FFN_IN][(number_in_group(sizes, me),) + spot] = from_ref[c, x].astype(jnp.float32)
            for step in range(1, reach(sizes, GROUP)):
                peer = peer_at(sizes, me, GROUP, step)
                shares[FFN_IN][(number_in_group(sizes, peer),) + spot] = into[step - 1].astype(
                    jnp.float32
                )
            return

        def one(step):
            here = pick(from_ref, before, level, me, step)[...]
            if last:
                here = here.astype(jnp.float32)
            for other in range(1, reach(sizes, level)):
                here = here + pick(into.at[other - 1], after, None, None, step)[...]
            return here

        if last:
            if number == total - 1:
                small_out[...] = one(None)
            else:
                which, block_rows, tall, wide, base = chunks[number]
                shares[which][pl.ds(row, tall_rows), pl.ds(base + column, columns)] = one(None)
        elif 0 in after:

            def body(step, carry):
                pick(into.at[0], after, None, None, step)[...] = one(step)
                return carry

            lax.fori_loop(0, far, body, 0)
        else:
            into[0] = one(None)

    def pass_on(number, stage):
        for unit in units_in[number]:
            for one in copies(unit, stage):
                one.wait_recv()
            add(unit, stage)
            if stage < 3:
                for one in copies(unit, stage + 1):
                    one.start()
        if stage == 1 and number in flats and flats.index(number) + flat_room < len(flats):
            sent(number, 1)
            for step in range(1, cores):
                pl.semaphore_signal(
                    credit,
                    inc=1,
                    device_id=device_at(sizes, moved(me, 2, lax.rem(c + step, cores))),
                    device_id_type=pl.DeviceIdType.MESH,
                )

    def produce(number, left, right):
        ref, previous = held(number)
        if previous is not None:
            sent(previous, 0)
        which, tall_rows, tall, wide, column = chunks[number]
        height = near * tall_rows if tall else slab
        right_value = right

        def body(step, carry):
            grad = product_left(left(step, height), right_value()).astype(jnp.bfloat16)
            into = ref.at[step]
            into[...] = grad.reshape(into.shape)
            return carry

        tiles(far, body)

    emitted = {}

    def emit(now, number, left=None, right=None):
        if left is not None:
            produce(number, left, right)
        start(number)
        emitted[number] = now

    def turn(now):
        for stage in (3, 2, 1, 0):
            for number, began in emitted.items():
                if began + 1 + LAG * stage == now:
                    pass_on(number, stage)

    def lanes_of(slot, height=1):
        def part(step, wide):
            if height == 1:
                return pool[slot, :, lane_tile(step, wide)]
            return pool[pl.ds(slot, height), :, lane_tile(step, wide)].reshape(height * amount, wide)

        return part

    def all_of(slot, height=1, wide=None):
        wide = width if wide is None else wide

        def part():
            if height == 1:
                return pool[slot, :, pl.ds(0, wide)]
            return pool[pl.ds(slot, height), :, pl.ds(0, wide)].reshape(height * amount, wide)

        return part

    fetch(SUM_THIRD, 0)
    fetch(CB, COTANGENT)
    fetch(VECTOR, 0)
    tall_copy().start()
    fetch(SLOPE, SLOPES, GROUP)
    weight_fetch(0)
    weight_fetch(1)
    fetch(ACTIVITY, ACTIVITIES, GROUP)
    fetch(SECOND_LOW, SECONDS, GROUP)
    wide_sums[...] = jnp.zeros_like(wide_sums)
    fetch(SUM_SECOND, 1)
    fetch(JOINED, JOINEDS)
    fetch(PROBE, PROBES)
    fetch(INDEX, INDEXES, 2)
    fetch(CONTENT, CONTENTS, 2)
    fetch(FIRST_LOW, FIRSTS)
    probs_copy(CROSS_P, 0, 0).start()
    probs_copy(SELF_P, 0, 0).start()
    sums[...] = jnp.zeros_like(sums)
    relative[...] = jnp.zeros_like(relative)
    enter(sizes, me)

    ready(SUM_THIRD, CB, VECTOR)
    norm_backward(full.at[0], GAIN_C, SHIFT_C, FFN_OUTB, pool.at[BRANCH_THREE], pool.at[COTANGENT])

    def to_item(item, source_slot, target_slot, number):
        return pltpu.make_async_remote_copy(
            src_ref=pool.at[source_slot],
            dst_ref=pool.at[target_slot],
            send_sem=pair_send.at[number],
            recv_sem=pair_recv.at[number],
            device_id=device_at(sizes, peer_at(sizes, me, GROUP, item)),
            device_id_type=pl.DeviceIdType.MESH,
        )

    branch_next = to_item(NEXT, BRANCH_THREE, BRANCH_THREE + NEXT, 0)
    branch_other = to_item(OTHER, BRANCH_THREE, BRANCH_THREE + OTHER, 1)
    branch_diagonal = to_item(OTHER, BRANCH_THREE + NEXT, BRANCH_THREE + DIAGONAL, 2)
    partial_other = to_item(OTHER, PARTIALS + OTHER, PARTIAL_OTHER, 3)
    partial_diagonal = to_item(OTHER, PARTIALS + DIAGONAL, PARTIAL_DIAGONAL, 4)
    partial_next = to_item(NEXT, PARTIALS + NEXT, PARTIAL_NEXT, 5)

    def slab_backward(item):
        feed_backward(item)
        left = all_of(SLOPES + item)
        if item == 0:
            through(FFN_IN, left, acc)
        else:
            through(FFN_IN, left, pool.at[PARTIALS + item], True)

    branch_next.start()
    branch_other.start()
    tall_copy().wait()
    ready(SLOPE)
    weight_ready(0)
    slab_backward(0)
    branch_other.wait()
    slab_backward(OTHER)
    partial_other.start()
    branch_next.wait_recv()
    branch_diagonal.start()
    ready(ACTIVITY, SECOND_LOW)
    fetch(SUM_FIRST, 0)

    def activity_lanes(step, wide):
        columns = lane_tile(step, wide)
        return pool[pl.ds(ACTIVITIES, GROUP), :, columns].reshape(GROUP * amount, wide)

    def third_lanes(part):
        wide = chunks[part][3]
        return lambda: pool[pl.ds(BRANCH_THREE, GROUP), :, pl.ds(part * wide, wide)].reshape(
            GROUP * amount, wide
        )

    def slab_lanes(part):
        wide = chunks[GROUP + part][3]
        return lambda: pool[pl.ds(SLOPES, GROUP), :, pl.ds(part * wide, wide)].reshape(
            GROUP * amount, wide
        )

    cross_places = (PROBES, INDEXES, CONTENTS, GRAD_JOINED, GRAD_PROBE, GRAD_INDEX, GRAD_CONTENT)
    self_places = (QUERIES, KEYSES, VALUESES, GRAD_MIXED, GRAD_QUERY, GRAD_KEYS, GRAD_VALUES)

    def second_backward():
        ready(SUM_SECOND, JOINED, PROBE, INDEX, CONTENT, FIRST_LOW)
        partial_other.wait()
        partial_next.wait()
        acc[...] += pool[PARTIAL_OTHER].astype(jnp.float32) + pool[PARTIAL_NEXT].astype(jnp.float32)
        norm_backward(full.at[1], GAIN_B, SHIFT_B, CROSS_OB, pool.at[BRANCH_TWO], None)
        back_through(CROSS_O, all_of(BRANCH_TWO), pool.at[GRAD_JOINED], True)

    def cross_backward(low):
        heads_backward(CROSS_P, low, low + pairs // 4, cross_places, source // amount)

    def first_backward():
        back_through(CROSS_Q, all_of(GRAD_PROBE), acc)
        ready(SUM_FIRST)
        norm_backward(full.at[0], GAIN_A, SHIFT_A, SELF_OB, pool.at[BRANCH_ONE], None)
        back_through(SELF_O, all_of(BRANCH_ONE), pool.at[GRAD_MIXED], True)

    def self_backward(low):
        if low == 0:
            ready(QUERY, KEYS, VALUES)
        heads_backward(SELF_P, low, low + pairs // 4, self_places, 1)

    step = pairs // 4
    slab_backward(NEXT)
    branch_diagonal.wait_recv()
    emit(0, 0, activity_lanes, third_lanes(0))
    slab_backward(DIAGONAL)
    weight_fetch(2)
    partial_diagonal.start()
    turn(0)
    emit(1, 1, activity_lanes, third_lanes(1))
    partial_diagonal.wait_recv()
    pool[PARTIALS + NEXT] = (
        pool[PARTIALS + NEXT].astype(jnp.float32) + pool[PARTIAL_DIAGONAL].astype(jnp.float32)
    ).astype(jnp.bfloat16)
    partial_next.start()
    for one in (branch_next, branch_diagonal, partial_diagonal):
        one.wait_send()
    turn(1)
    emit(2, 2, activity_lanes, third_lanes(2))
    turn(2)
    emit(3, 3, activity_lanes, third_lanes(3))
    turn(3)
    emit(4, 4, lanes_of(SECONDS, GROUP), slab_lanes(0))
    second_backward()
    turn(4)
    emit(5, 5, lanes_of(SECONDS, GROUP), slab_lanes(1))
    cross_backward(0)
    turn(5)
    emit(6, 6, lanes_of(SECONDS, GROUP), slab_lanes(2))
    cross_backward(step)
    turn(6)
    emit(7, 7, lanes_of(SECONDS, GROUP), slab_lanes(3))
    fetch(EB, ENCODED, 2)
    fetch(QUERY, QUERIES)
    fetch(MIXED, MIXEDS)
    cross_backward(2 * step)
    turn(7)
    emit(8, 8, lanes_of(JOINEDS), all_of(BRANCH_TWO))
    fetch(KEYS, KEYSES)
    cross_backward(3 * step)
    fetch(VALUES, VALUESES)
    fetch(RB, TOKENS)
    turn(8)
    emit(9, 9, lanes_of(FIRSTS), all_of(GRAD_PROBE))
    first_backward()
    turn(9)
    ready(EB)
    emit(10, 10, lanes_of(ENCODED, 2), all_of(GRAD_CONTENT, 2))
    self_backward(0)
    turn(10)
    emit(11, 11, lanes_of(ENCODED, 2), all_of(GRAD_INDEX, 2))
    self_backward(step)
    turn(11)
    ready(MIXED)
    emit(12, 12, lanes_of(MIXEDS), all_of(BRANCH_ONE))
    self_backward(2 * step)
    turn(12)
    self_backward(3 * step)
    ready(RB)
    now = 13
    pool[GRAD_RELATIVE, :, pl.ds(0, relative.shape[1])] = relative[...].astype(jnp.bfloat16)
    sums[pl.ds(row_of(BUCKET_B), 1), pl.ds(0, relative.shape[1])] = jnp.sum(
        relative[...].astype(jnp.bfloat16).astype(jnp.float32), axis=0, keepdims=True
    )
    fits = devices * 128 // width
    for index in range(devices):
        spot = (
            index // (side * cores * near),
            index // (side * cores) % near,
            index // side % cores,
            index % side,
        )
        small[spot] = sums[:, pl.ds(index // fits * 128, 128)]
        block = index * relative.shape[1] // (devices * 128)
        small[spot + (pl.ds(row_of(BUCKET_B), 1),)] = sums[
            pl.ds(row_of(BUCKET_B), 1), pl.ds(block * 128, 128)
        ]
    for index in range(far * near):
        spot = (index // near, index % near, c, x)
        small[spot + (pl.ds(row_of(FFN_INB), 1),)] = wide_sums[:, pl.ds(index * 128, 128)]
    emit(now, 17)
    last = (
        (13, GRAD_VALUES, width),
        (14, GRAD_KEYS, width),
        (15, GRAD_QUERY, width),
        (16, GRAD_RELATIVE, relative.shape[1]),
    )
    for number, grads, wide in last:
        emit(now, number, lanes_of(TOKENS), all_of(grads, 1, wide))
        turn(now)
        now += 1

    def encoded_part(which, slot, fresh):
        number = order.index(which)
        weight_ready(number)

        def body(step, carry):
            columns = lane_tile(step, slab)
            piece = low_slot[number % 2, step].reshape(slab, width)
            result = product_right(all_of(slot, 2)(), piece)
            for part in range(source // amount):
                lines = result[part * amount : (part + 1) * amount]
                if fresh:
                    full[part, :, columns] = lines
                else:
                    full[part, :, columns] += lines
            return carry

        tiles(far, body)
        weight_fetch(number + 2)

    drain = [
        lambda: encoded_part(CROSS_K, GRAD_INDEX, True),
        lambda: encoded_part(CROSS_V, GRAD_CONTENT, False),
        lambda: back_through(SELF_Q, all_of(GRAD_QUERY), acc),
        lambda: back_through(SELF_K, all_of(GRAD_KEYS), acc),
        lambda: back_through(SELF_V, all_of(GRAD_VALUES), acc),
        lambda: back_through(BUCKET_W, all_of(GRAD_RELATIVE, 1, relative.shape[1]), acc),
    ]
    results = [
        pltpu.make_async_copy(
            full.at[part], encoded_out.at[pl.ds(part * amount, amount)], out_sem.at[part]
        )
        for part in range(source // amount)
    ]
    results.append(pltpu.make_async_copy(acc, tokens_out, out_sem.at[len(results)]))
    end = max(emitted.values()) + 1 + 3 * LAG
    piece = 0
    while now <= end or piece < len(drain):
        if piece < len(drain):
            drain[piece]()
            piece += 1
            if piece == 2:
                for one in results[:-1]:
                    one.start()
            if piece == len(drain):
                results[-1].start()
        turn(now)
        now += 1
    for number in range(total):
        for stage in range(4):
            sent(number, stage)
    for one in results:
        one.wait()


def backward_all(sizes, whole, kept, rows, enc, cotangent, buckets, valid):
    devices = sizes[0] * sizes[1] * sizes[2] * sizes[3]
    chunks = []
    for which in SUM_ORDER:
        parts, tall_rows, wide = whole[which].shape[0], whole[which].shape[-2], whole[which].shape[-1]
        for part in range(parts):
            chunks.append((which, tall_rows, tall_rows > ROWS, wide, part * wide))
    flat_room, low, full = 6, jnp.bfloat16, jnp.float32
    amount, width = rows.shape
    wide_rows, tall_wide = whole[FFN_OUT].shape[-2:]
    hidden_units = wide_rows * devices // GROUP
    buckets_wide = whole[BUCKET_W].shape[-1]
    far, near, cores, side = sizes
    inbox = []
    total = 0
    for number in range(len(chunks) + 1):
        summed = number < len(chunks)
        block = (chunks[number][1], chunks[number][3]) if summed else (16, 128)
        kind = low if summed else full
        which = chunks[number][0] if summed else -1
        for row, tall_rows, column, columns, route in units_of(which, *block):
            total += 1
            left = levels_of(which)
            for stage, level in enumerate(sum_route(which, route)):
                left = without(left, (level,))
                if stage > 0 or which in (FFN_IN, FFN_OUT, -1):
                    shape = (reach(sizes, level) - 1,) + tuple(sizes[one] for one in left)
                    inbox.append(pltpu.VMEM(shape + (tall_rows, columns), kind))
    unused, places = slots(sizes)
    any_spec = pl.BlockSpec(memory_space=pl.ANY)
    vmem_spec = pl.BlockSpec(memory_space=pltpu.VMEM)
    shapes = []
    for which in MATRICES:
        shape = (whole[which].shape[-2], whole[which].shape[0] * whole[which].shape[-1])
        if which == FFN_IN:
            shape = (GROUP,) + shape
        shapes.append(jax.ShapeDtypeStruct(shape, full))
    results = pl.pallas_call(
        partial(backward_kernel, sizes, chunks, flat_room),
        out_shape=[jax.ShapeDtypeStruct((16, 128), full)]
        + shapes
        + [jax.ShapeDtypeStruct(rows.shape, full), jax.ShapeDtypeStruct(enc.shape, full)],
        in_specs=[any_spec, vmem_spec, vmem_spec] + [any_spec] * (2 + len(SAVED) + len(MATRICES)),
        out_specs=[vmem_spec] * (1 + len(MATRICES)) + [any_spec] * 2,
        scratch_shapes=[
            pltpu.VMEM((POOL, amount, width), low),
            pltpu.VMEM((2, amount, width), full),
            pltpu.VMEM((amount, width), full),
            pltpu.VMEM((16, width), full),
            pltpu.VMEM((16, width), full),
            pltpu.VMEM((1, hidden_units), full),
            pltpu.VMEM(sizes + (16, 128), full),
            pltpu.VMEM((amount, buckets_wide), full),
            pltpu.VMEM((2, amount, amount // 2), full),
            pltpu.VMEM((2, amount, max(amount, enc.shape[0])), full),
            pltpu.VMEM((2, amount, max(amount, enc.shape[0])), low),
            pltpu.VMEM((2,) + sizes + (ROWS, WIDE), low),
            pltpu.VMEM(whole[FFN_OUT].shape, low),
            pltpu.VMEM((2,) + kept[SELF_P].shape[1:], low),
            pltpu.VMEM((2,) + kept[CROSS_P].shape[1:], low),
            pltpu.VMEM((3,) + sizes + (ROWS, WIDE), low),
            pltpu.VMEM((2, far, near, wide_rows, tall_wide), low),
            pltpu.VMEM((flat_room, far, near, side, ROWS, WIDE), low),
        ]
        + inbox
        + [
            pltpu.SemaphoreType.DMA((32,)),
            pltpu.SemaphoreType.DMA((2 * GROUP + 1,)),
            pltpu.SemaphoreType.DMA((2,)),
            pltpu.SemaphoreType.DMA((2,)),
            pltpu.SemaphoreType.DMA((1 + enc.shape[0] // amount,)),
            pltpu.SemaphoreType.REGULAR,
            pltpu.SemaphoreType.DMA((6,)),
            pltpu.SemaphoreType.DMA((6,)),
            pltpu.SemaphoreType.DMA((total, places)),
            pltpu.SemaphoreType.DMA((total, places)),
        ],
        compiler_params=pltpu.CompilerParams(
            collective_id=1,
            has_side_effects=True,
            vmem_limit_bytes=63 * 1024 * 1024,
            fuse_transposed_lhs_in_matmul=True,
        ),
        cost_estimate=pl.CostEstimate(flops=2 * 10**10, bytes_accessed=1 << 27, transcendentals=0),
        name="backward_all",
    )(
        cotangent,
        buckets,
        valid,
        rows,
        enc,
        *[kept[name] for name in SAVED],
        *[whole[name] for name in MATRICES],
    )
    return results[0], results[1 : 1 + len(MATRICES)], results[-2], results[-1]


def finish_kernel(count, *refs):
    ins, outs, sem = refs[:count], refs[count : 2 * count], refs[2 * count]
    copies = [pltpu.make_async_copy(ins[one], outs[one], sem.at[one]) for one in range(count)]
    for one in copies:
        one.start()
    for one in copies:
        one.wait()


def finish(arrays):
    return pl.pallas_call(
        partial(finish_kernel, len(arrays)),
        out_shape=[jax.ShapeDtypeStruct(array.shape, array.dtype) for array in arrays],
        in_specs=[pl.BlockSpec(memory_space=pl.ANY)] * len(arrays),
        out_specs=[pl.BlockSpec(memory_space=pltpu.VMEM)] * len(arrays),
        scratch_shapes=[pltpu.SemaphoreType.DMA((len(arrays),))],
        name="finish",
    )(*arrays)


def quarters(sizes, block):
    split = block.reshape(block.shape[0], sizes[0] * sizes[1], GROUP, -1)
    return split.transpose(2, 0, 1, 3).reshape(GROUP, block.shape[0], -1)


def own_index():
    return lax.axis_index(AXES[0]) * lax.psum(1, AXES[1]) + lax.axis_index(AXES[1])


def spread_small(params):
    lane = lax.broadcasted_iota(jnp.int32, (1, 128), 1)
    index = own_index()
    rows = []
    for names in (VECTORS,) + tuple((name,) for name in NARROW[len(VECTORS) :]):
        width = params[names[0]].shape[0]
        fits = 128 // width
        block = jnp.tile(jnp.stack([params[name] for name in names]), (1, fits))
        rows.append(jnp.where(lane // width == lax.rem(index, fits), block, 0))
    rows.append(jnp.zeros((16 - len(NARROW), 128), rows[0].dtype))
    return jnp.concatenate(rows)


def deliver(pairs, sums):
    grads = dict(sums)
    for name in MATRICES:
        grads[name] = product_left(*pairs[name])
    return tuple(
        lax.psum_scatter(grads[name], AXES, scatter_dimension=0, tiled=True) for name in WHOLE
    )


def product(left, right):
    return jnp.dot(left, right, preferred_element_type=jnp.float32)


def product_left(left, right):
    return lax.dot_general(
        left, right, (((0,), (0,)), ((), ())), preferred_element_type=jnp.float32
    )


def product_right(left, right):
    return lax.dot_general(
        left, right, (((1,), (1,)), ((), ())), preferred_element_type=jnp.float32
    )


def column_sum(grad):
    return jnp.sum(grad.astype(jnp.float32), axis=0)


def layer_norm(summed, gain, shift):
    center = summed - jnp.mean(summed, axis=-1, keepdims=True)
    spread = jnp.mean(center * center, axis=-1, keepdims=True)
    return center * lax.rsqrt(spread + 1e-05) * gain.astype(jnp.float32) + shift.astype(jnp.float32)


def norm_back(summed, gain, shift, grad):
    unused, pull = jax.vjp(layer_norm, summed, gain.astype(jnp.float32), shift.astype(jnp.float32))
    return pull(grad)


def visible(target):
    place = jnp.arange(2 * target, dtype=jnp.int32) % target
    stream = jnp.arange(2 * target, dtype=jnp.int32) // target
    row_place = place[:, None]
    key_place = place[None, :]
    row_stream = stream[:, None]
    key_stream = stream[None, :]
    earlier = (key_stream == 0) & (
        (row_stream == 0) & (key_place <= row_place) | (row_stream == 1) & (key_place < row_place)
    )
    itself = (key_stream == 1) & (row_stream == 1) & (key_place == row_place)
    return earlier | itself


def valid_rows(lengths, target):
    valid = (jnp.arange(target, dtype=jnp.int32)[None, :] < lengths[:, None]).astype(jnp.float32)
    return jnp.concatenate([valid, valid], axis=1).reshape(-1)


def bucket_table(buckets):
    count, streams, target, width = buckets.shape
    flat = buckets.reshape(count, streams * target, width)
    return (
        flat[:, :, None, :] == jnp.arange(BUCKETS, dtype=jnp.int32)[None, None, :, None]
    ).astype(jnp.float32)


def relative_bias(onehot, relative):
    table = relative.reshape(onehot.shape[0], onehot.shape[1], -1, BUCKETS)
    return jnp.einsum("nqbk,nqhb->nhqk", onehot, table, precision=lax.Precision.HIGHEST)


def scores_of(query, keys, bias, allowed):
    scores = (
        jnp.einsum("nqhd,nkhd->nhqk", query, keys, preferred_element_type=jnp.float32) * 0.125
        + bias
    )
    return jnp.where(allowed, scores, -1e30)


def attend(query, keys, values, bias, allowed):
    scores = scores_of(query, keys, bias, allowed)
    top = jnp.max(scores, axis=-1, keepdims=True)
    logsum = top + jnp.log(jnp.sum(jnp.exp(scores - top), axis=-1, keepdims=True))
    probs = jnp.exp(scores - logsum).astype(jnp.bfloat16)
    mixed = jnp.einsum("nhqk,nkhd->nqhd", probs, values, preferred_element_type=jnp.float32)
    return (mixed.astype(jnp.bfloat16), logsum)


def attend_back(query, keys, values, bias, allowed, logsum, grad_out):
    probs = jnp.exp(scores_of(query, keys, bias, allowed) - logsum)
    grad_probs = jnp.einsum("nqhd,nkhd->nhqk", grad_out, values, preferred_element_type=jnp.float32)
    grad_scores = (
        probs * (grad_probs - jnp.sum(probs * grad_probs, axis=-1, keepdims=True))
    ).astype(jnp.bfloat16)
    grad_query = (
        jnp.einsum("nhqk,nkhd->nqhd", grad_scores, keys, preferred_element_type=jnp.float32) * 0.125
    ).astype(jnp.bfloat16)
    grad_keys = (
        jnp.einsum("nhqk,nqhd->nkhd", grad_scores, query, preferred_element_type=jnp.float32)
        * 0.125
    ).astype(jnp.bfloat16)
    grad_values = jnp.einsum(
        "nhqk,nqhd->nkhd", probs.astype(jnp.bfloat16), grad_out, preferred_element_type=jnp.float32
    ).astype(jnp.bfloat16)
    return (grad_scores, grad_query, grad_keys, grad_values)


def forward(whole, tokens, encoded, buckets):
    (
        self_q,
        self_qb,
        self_k,
        self_v,
        self_vb,
        self_o,
        self_ob,
        bucket_w,
        bucket_b,
        cross_q,
        cross_qb,
        cross_k,
        cross_v,
        cross_vb,
        cross_o,
        cross_ob,
        ffn_in,
        ffn_inb,
        ffn_out,
        ffn_outb,
        gain_a,
        shift_a,
        gain_b,
        shift_b,
        gain_c,
        shift_c,
    ) = whole
    count, streams, target, width = tokens.shape
    source = encoded.shape[1]
    head_shape = (count, streams * target, width // HEAD_DIM, HEAD_DIM)
    source_shape = (count, source, width // HEAD_DIM, HEAD_DIM)
    rows = tokens.reshape(-1, width)
    enc_rows = encoded.reshape(-1, width)
    allowed = visible(target)
    query = (product(rows, self_q) + self_qb).astype(jnp.bfloat16)
    keys = product(rows, self_k).astype(jnp.bfloat16)
    values = (product(rows, self_v) + self_vb).astype(jnp.bfloat16)
    relative = product(rows, bucket_w) + bucket_b
    bias = relative_bias(bucket_table(buckets), relative)
    mixed, logsum = attend(
        query.reshape(head_shape),
        keys.reshape(head_shape),
        values.reshape(head_shape),
        bias,
        allowed,
    )
    mixed = mixed.reshape(rows.shape)
    sum_first = rows + product(mixed, self_o) + self_ob
    first = layer_norm(sum_first, gain_a, shift_a)
    first_low = first.astype(jnp.bfloat16)
    probe = (product(first_low, cross_q) + cross_qb).astype(jnp.bfloat16)
    index = product(enc_rows, cross_k).astype(jnp.bfloat16)
    content = (product(enc_rows, cross_v) + cross_vb).astype(jnp.bfloat16)
    joined, cross_logsum = attend(
        probe.reshape(head_shape),
        index.reshape(source_shape),
        content.reshape(source_shape),
        0.0,
        True,
    )
    joined = joined.reshape(rows.shape)
    sum_second = first + product(joined, cross_o) + cross_ob
    second = layer_norm(sum_second, gain_b, shift_b)
    second_low = second.astype(jnp.bfloat16)
    before = product(second_low, ffn_in) + ffn_inb
    activity = jax.nn.gelu(before, approximate=False).astype(jnp.bfloat16)
    sum_third = second + product(activity, ffn_out) + ffn_outb
    third = layer_norm(sum_third, gain_c, shift_c)
    kept = (
        rows,
        enc_rows,
        query,
        keys,
        values,
        relative,
        logsum,
        mixed,
        sum_first,
        first_low,
        probe,
        index,
        content,
        cross_logsum,
        joined,
        sum_second,
        second_low,
        before,
        activity,
        sum_third,
    )
    return (third, kept)


def backward(whole, kept, cotangent, buckets, lengths):
    (
        self_q,
        self_qb,
        self_k,
        self_v,
        self_vb,
        self_o,
        self_ob,
        bucket_w,
        bucket_b,
        cross_q,
        cross_qb,
        cross_k,
        cross_v,
        cross_vb,
        cross_o,
        cross_ob,
        ffn_in,
        ffn_inb,
        ffn_out,
        ffn_outb,
        gain_a,
        shift_a,
        gain_b,
        shift_b,
        gain_c,
        shift_c,
    ) = whole
    (
        rows,
        enc_rows,
        query,
        keys,
        values,
        relative,
        logsum,
        mixed,
        sum_first,
        first_low,
        probe,
        index,
        content,
        cross_logsum,
        joined,
        sum_second,
        second_low,
        before,
        activity,
        sum_third,
    ) = kept
    count, streams, target, width = cotangent.shape
    source = enc_rows.shape[0] // count
    head_shape = (count, streams * target, width // HEAD_DIM, HEAD_DIM)
    source_shape = (count, source, width // HEAD_DIM, HEAD_DIM)
    allowed = visible(target)
    grad_third = (
        cotangent.reshape(rows.shape).astype(jnp.float32) * valid_rows(lengths, target)[:, None]
    )
    grad_sum_third, grad_gain_c, grad_shift_c = norm_back(sum_third, gain_c, shift_c, grad_third)
    branch_three = grad_sum_third.astype(jnp.bfloat16)
    pair_ffn_out = (activity, branch_three)
    grad_ffn_outb = column_sum(branch_three)
    unused, gelu_pull = jax.vjp(partial(jax.nn.gelu, approximate=False), before)
    grad_before = gelu_pull(product_right(branch_three, ffn_out))[0].astype(jnp.bfloat16)
    pair_ffn_in = (second_low, grad_before)
    grad_ffn_inb = column_sum(grad_before)
    grad_second = grad_sum_third + product_right(grad_before, ffn_in)
    grad_sum_second, grad_gain_b, grad_shift_b = norm_back(sum_second, gain_b, shift_b, grad_second)
    branch_two = grad_sum_second.astype(jnp.bfloat16)
    pair_cross_o = (joined, branch_two)
    grad_cross_ob = column_sum(branch_two)
    grad_joined = product_right(branch_two, cross_o).astype(jnp.bfloat16)
    unused, grad_probe, grad_index, grad_content = attend_back(
        probe.reshape(head_shape),
        index.reshape(source_shape),
        content.reshape(source_shape),
        0.0,
        True,
        cross_logsum,
        grad_joined.reshape(head_shape),
    )
    grad_probe = grad_probe.reshape(rows.shape)
    grad_index = grad_index.reshape(enc_rows.shape)
    grad_content = grad_content.reshape(enc_rows.shape)
    pair_cross_q = (first_low, grad_probe)
    grad_cross_qb = column_sum(grad_probe)
    pair_cross_k = (enc_rows, grad_index)
    pair_cross_v = (enc_rows, grad_content)
    grad_cross_vb = column_sum(grad_content)
    grad_encoded = product_right(grad_index, cross_k) + product_right(grad_content, cross_v)
    grad_first = grad_sum_second + product_right(grad_probe, cross_q)
    grad_sum_first, grad_gain_a, grad_shift_a = norm_back(sum_first, gain_a, shift_a, grad_first)
    branch_one = grad_sum_first.astype(jnp.bfloat16)
    pair_self_o = (mixed, branch_one)
    grad_self_ob = column_sum(branch_one)
    grad_mixed = product_right(branch_one, self_o).astype(jnp.bfloat16)
    onehot = bucket_table(buckets)
    bias = relative_bias(onehot, relative)
    grad_scores, grad_query, grad_keys, grad_values = attend_back(
        query.reshape(head_shape),
        keys.reshape(head_shape),
        values.reshape(head_shape),
        bias,
        allowed,
        logsum,
        grad_mixed.reshape(head_shape),
    )
    grad_relative = jnp.einsum(
        "nqbk,nhqk->nqhb", onehot, grad_scores.astype(jnp.float32), precision=lax.Precision.HIGHEST
    )
    grad_relative = grad_relative.reshape(rows.shape[0], -1).astype(jnp.bfloat16)
    grad_query = grad_query.reshape(rows.shape)
    grad_keys = grad_keys.reshape(rows.shape)
    grad_values = grad_values.reshape(rows.shape)
    pair_self_q = (rows, grad_query)
    grad_self_qb = column_sum(grad_query)
    pair_self_k = (rows, grad_keys)
    pair_self_v = (rows, grad_values)
    grad_self_vb = column_sum(grad_values)
    pair_bucket_w = (rows, grad_relative)
    grad_bucket_b = column_sum(grad_relative)
    grad_tokens = (
        grad_sum_first
        + product_right(grad_query, self_q)
        + product_right(grad_keys, self_k)
        + product_right(grad_values, self_v)
        + product_right(grad_relative, bucket_w)
    )
    pairs = (
        pair_self_q,
        pair_self_k,
        pair_self_v,
        pair_bucket_w,
        pair_self_o,
        pair_cross_k,
        pair_cross_v,
        pair_cross_q,
        pair_cross_o,
        pair_ffn_in,
        pair_ffn_out,
    )
    sums = (
        grad_self_qb,
        grad_self_vb,
        grad_self_ob,
        grad_cross_qb,
        grad_cross_vb,
        grad_cross_ob,
        grad_ffn_outb,
        grad_gain_a,
        grad_shift_a,
        grad_gain_b,
        grad_shift_b,
        grad_gain_c,
        grad_shift_c,
        grad_bucket_b,
        grad_ffn_inb,
    )
    return (
        dict(zip(MATRICES, pairs)),
        dict(zip(NARROW, sums)),
        grad_tokens.reshape(cotangent.shape),
        grad_encoded.reshape(count, source, width),
    )


def per_device(mesh_shape, tokens, encoded, cotangent, buckets, lengths, *shards):
    params = dict(zip(WHOLE, shards))
    dp, fsdp = mesh_shape
    sizes = chips(dp, fsdp)
    valid = valid_rows(lengths, tokens.shape[2])[:, None]
    if any(params[name].shape[0] % ROWS for name in MATRICES):
        whole = tuple(lax.all_gather(params[name], AXES, axis=0, tiled=True) for name in WHOLE)
        third, kept = forward(whole, tokens, encoded, buckets)
        outputs = (third * valid).astype(jnp.bfloat16)
        pairs, sums, grad_tokens, grad_encoded = backward(whole, kept, cotangent, buckets, lengths)
        shares = deliver(pairs, sums)
    else:
        rows = tokens.reshape(-1, tokens.shape[-1])
        enc_rows = encoded.reshape(-1, encoded.shape[-1])
        table = buckets.reshape(rows.shape[0], -1)
        outputs, whole, kept = forward_all(
            sizes,
            spread_small(params),
            [
                quarters(sizes, params[name]) if name == FFN_IN else params[name]
                for name in MATRICES
            ],
            rows,
            enc_rows,
            table,
            valid,
        )
        small, own, grad_tokens, grad_encoded = backward_all(
            sizes, whole, kept, rows, enc_rows, cotangent.reshape(rows.shape), table, valid
        )
        plain = [one for one, name in zip(own, MATRICES) if name != FFN_IN]
        outputs, grad_tokens, grad_encoded, *plain = finish(
            [outputs, grad_tokens, grad_encoded] + plain
        )
        out = dict(zip([name for name in MATRICES if name != FFN_IN], plain))
        grad = own[MATRICES.index(FFN_IN)]
        grad = grad.reshape(GROUP, grad.shape[1], sizes[0] * sizes[1], -1)
        out[FFN_IN] = grad.transpose(1, 2, 0, 3).reshape(params[FFN_IN].shape)
        index = own_index()
        for row, name in enumerate(NARROW):
            width = params[name].shape[0]
            at = lax.rem(index, 128 // width) * width
            out[name] = lax.dynamic_slice(small, (row, at), (1, width)).reshape(width)
        shares = tuple(out[name] for name in WHOLE)
    return (
        outputs.reshape(tokens.shape),
        grad_tokens.reshape(tokens.shape),
        grad_encoded.reshape(encoded.shape),
    ) + shares


def solution(mesh):
    def split(ranks):
        return tuple(P(AXES, *[None] * (rank - 1)) for rank in ranks)

    ranks = tuple(1 if name in NARROW else 2 for name in WHOLE)
    return jax.shard_map(
        partial(per_device, (mesh.shape[AXES[0]], mesh.shape[AXES[1]])),
        mesh=mesh,
        in_specs=split((4, 3, 4, 4, 1) + ranks),
        out_specs=split((4, 4, 3) + ranks),
        check_vma=False,
    )
```

```python
from functools import partial

import jax
import jax.numpy as jnp
from jax import lax
from jax.experimental import pallas as pl
from jax.experimental.pallas import tpu as pltpu
from jax.sharding import PartitionSpec as P

HEAD_DIM = 64
BUCKETS = 32
CORES = 2
ROWS = 32
WIDE = 1024
AHEAD = 3
LINES = 64
LAG = 2
GATHER_LAG = 1
AXES = ("dp", "fsdp")
(
    SELF_Q, SELF_K, SELF_V, BUCKET_W, SELF_O, CROSS_K,
    CROSS_V, CROSS_Q, CROSS_O, FFN_IN, FFN_OUT,
) = MATRICES = tuple(range(11))
(
    SELF_QB, SELF_VB, SELF_OB, CROSS_QB, CROSS_VB, CROSS_OB,
    FFN_OUTB, GAIN_A, SHIFT_A, GAIN_B, SHIFT_B, GAIN_C,
    SHIFT_C, BUCKET_B, FFN_INB,
) = NARROW = tuple(range(11, 26))
VECTORS = NARROW[:13]
WHOLE = (
    SELF_Q, SELF_QB, SELF_K, SELF_V, SELF_VB, SELF_O,
    SELF_OB, BUCKET_W, BUCKET_B, CROSS_Q, CROSS_QB, CROSS_K,
    CROSS_V, CROSS_VB, CROSS_O, CROSS_OB, FFN_IN, FFN_INB,
    FFN_OUT, FFN_OUTB, GAIN_A, SHIFT_A, GAIN_B, SHIFT_B,
    GAIN_C, SHIFT_C,
)
(
    QUERY, KEYS, VALUES, MIXED, FIRST_LOW, PROBE,
    JOINED, SECOND_LOW, INDEX, CONTENT, SUM_FIRST, SUM_SECOND,
    SUM_THIRD, SLOPE, ACTIVITY, SELF_P, CROSS_P, VECTOR,
) = SAVED = tuple(range(18))


RB, EB, CB = 18, 19, 20
SUM_ORDER = (
    FFN_OUT, FFN_IN, CROSS_O, CROSS_Q, CROSS_V, CROSS_K, SELF_O, SELF_V, SELF_K, SELF_Q, BUCKET_W,
)
POOL = 32
ACTIVITIES, SLOPES, COTANGENT, BRANCH_THREE, SECONDS, JOINEDS, PROBES = 0, 4, 8, 9, 13, 17, 18
INDEXES, CONTENTS, FIRSTS = 19, 21, 23
BRANCH_TWO, GRAD_JOINED, GRAD_PROBE, GRAD_INDEX, GRAD_CONTENT, ENCODED = 8, 0, 1, 2, 24, 6
MIXEDS, QUERIES, KEYSES, VALUESES, TOKENS = 9, 10, 17, 18, 19
BRANCH_ONE, GRAD_MIXED, GRAD_QUERY, GRAD_KEYS, GRAD_VALUES, GRAD_RELATIVE = 20, 21, 22, 0, 8, 23
PARTIALS, PARTIAL_OTHER, PARTIAL_DIAGONAL, PARTIAL_NEXT = 25, 29, 30, 31
GATHER_ORDER = (
    SELF_Q, SELF_K, SELF_V, BUCKET_W, SELF_O, CROSS_Q, CROSS_K, CROSS_V,
    CROSS_O, FFN_IN, FFN_IN, FFN_IN, FFN_IN, FFN_OUT, FFN_OUT, FFN_OUT, FFN_OUT,
)
GROUP = 4
NEXT, OTHER, DIAGONAL = 1, 2, 3


def chips(dp, fsdp):
    square = fsdp
    return (dp // (CORES * square), square, CORES, fsdp)


def place(sizes):
    far, near, cores, side = sizes
    row = lax.axis_index(AXES[0])
    return (row // (near * cores), lax.rem(row // cores, near), lax.rem(row, cores), lax.axis_index(AXES[1]))


def device_at(sizes, spot):
    z, y, c, x = spot
    return ((z * sizes[1] + y) * sizes[2] + c, x)


def moved(spot, level, digit):
    return spot[:level] + (digit,) + spot[level + 1 :]


def peer_at(sizes, me, level, step):
    if level < GROUP:
        return moved(me, level, lax.rem(me[level] + step, sizes[level]))
    core = lax.rem(me[2] + step // sizes[3], sizes[2])
    return (me[0], me[1], core, lax.rem(me[3] + step % sizes[3], sizes[3]))


def reach(sizes, level):
    return sizes[level] if level < GROUP else sizes[2] * sizes[3]


def number_in_group(sizes, spot):
    return spot[2] * sizes[3] + spot[3]


def enter(sizes, me):
    barrier = pltpu.get_barrier_semaphore()
    peers = [(level, step) for level in range(GROUP) for step in range(1, sizes[level])]
    peers += [
        (GROUP, step) for step in range(sizes[3] + 1, sizes[2] * sizes[3]) if step % sizes[3]
    ]
    for level, step in peers:
        pl.semaphore_signal(
            barrier,
            inc=1,
            device_id=device_at(sizes, peer_at(sizes, me, level, step)),
            device_id_type=pl.DeviceIdType.MESH,
        )
    pl.semaphore_wait(barrier, len(peers))


ROUTES = ((0, 1, 3, 2), (0, 3, 1, 2), (3, 1, 0, 2))


def levels_of(which):
    return (0, 1) if which == FFN_OUT else (0, 1, 2, 3)


def gather_route(which, route):
    if which == FFN_OUT:
        return (0, 1)
    return (GROUP, 0, 1) if which == FFN_IN else ROUTES[route]


def sum_route(which, route):
    if which == FFN_OUT:
        return (1, 0)
    return (1, 0, GROUP) if which == FFN_IN else (2,) + ROUTES[route][2::-1]


def without(levels, done):
    gone = tuple(done) + ((2, 3) if GROUP in done else ())
    return tuple(level for level in levels if level not in gone)


def units_of(which, rows, columns):
    if which in (-1, FFN_IN, FFN_OUT) or columns % 256:
        return [(0, rows, 0, columns, 0)]
    half = columns // 2
    return [(0, rows, 0, half, 0), (0, rows, half, half, 1)]


def slots(sizes):
    first = []
    total = 0
    for level in range(GROUP + 1):
        first.append(total)
        total += reach(sizes, level) - 1
    return first, total


def parts_of(devices, which, shape):
    rows, columns = shape[-2:]
    wide = min(columns, WIDE * ROWS // rows)
    if which == FFN_IN:
        wide = WIDE // GROUP
    return (rows, wide), columns // wide


def lane_tile(step, wide):
    if isinstance(step, int):
        return pl.ds(step * wide, wide)
    return pl.ds(pl.multiple_of(step * wide, wide), wide)


def tiles(count, body):
    for step in range(count):
        body(step, 0)


def normal(summed, gain, shift):
    center = summed - jnp.mean(summed, axis=-1, keepdims=True)
    spread = jnp.mean(center * center, axis=-1, keepdims=True)
    return center * lax.rsqrt(spread + 1e-05) * gain + shift


def softmax_rows(scores):
    weights = jnp.exp(scores - jnp.max(scores, axis=-1, keepdims=True))
    return weights * (1.0 / jnp.sum(weights, axis=-1, keepdims=True))


def forward_kernel(sizes, chunks, saved, *refs):
    far, near, cores, side = sizes
    devices = far * near * cores * side
    count = len(MATRICES)
    rows, enc, buckets, valid, small = refs[:5]
    shards, refs = refs[5 : 5 + count], refs[5 + count :]
    outputs, refs = refs[0], refs[1:]
    whole, refs = refs[:count], refs[count:]
    kept, refs = refs[: len(saved)], refs[len(saved) :]
    held = dict(zip(saved, refs[: len(saved)]))
    refs = refs[len(saved) :]
    here, refs = refs[:count], refs[count:]
    vectors, relative, hidden, first, second, wide_bias, partial_out, partial_in, room = refs[:9]
    kept_sem, whole_sem, pair_send, pair_recv, own_sem, send_sem, recv_sem = refs[9:]
    vector = held[VECTOR]
    me = place(sizes)
    slot_of, unused = slots(sizes)
    total = len(chunks)
    units = []
    units_in = []
    for number, (which, part, tall, wide) in enumerate(chunks):
        block_rows = small.shape[0] if which < 0 else whole[which].shape[-2]
        own_units = [(number,) + unit for unit in units_of(which, block_rows, wide)]
        units_in.append(range(len(units), len(units) + len(own_units)))
        units += own_units

    def region(unit, spot, done):
        number, row, tall_rows, column, columns, route = units[unit]
        which, part, tall, wide = chunks[number]
        stay = without(levels_of(which), done)
        index = tuple(
            spot[level] if level in stay else slice(None) for level in levels_of(which)
        )
        if which < 0:
            return vectors.at[index]
        return here[which].at[(part,) + index + (pl.ds(row, tall_rows), pl.ds(column, columns))]

    def own(unit, spot):
        number, row, tall_rows, column, columns, route = units[unit]
        which, part, tall, wide = chunks[number]
        if which < 0:
            return small
        shard = shards[which]
        if which == FFN_IN:
            shard = shard.at[number_in_group(sizes, spot)]
        return shard.at[pl.ds(row, tall_rows), pl.ds(part * wide + column, columns)]

    def route_of(unit):
        return gather_route(chunks[units[unit][0]][0], units[unit][-1])

    def copy(unit, stage, step, from_peer):
        order = route_of(unit)
        level = order[stage]
        size = reach(sizes, level)
        done = order[:stage]
        slot = slot_of[level] + step - 1
        if from_peer:
            peer = peer_at(sizes, me, level, step if level == GROUP else size - step)
            target = region(unit, peer, done)
            source = target
        else:
            peer = peer_at(sizes, me, level, step)
            target = region(unit, me, done)
            source = own(unit, peer) if level == GROUP else target
        return pltpu.make_async_remote_copy(
            src_ref=source,
            dst_ref=target,
            send_sem=send_sem.at[unit, slot],
            recv_sem=recv_sem.at[unit, slot],
            device_id=device_at(sizes, peer),
            device_id_type=pl.DeviceIdType.MESH,
        )

    def steps(unit, stage):
        order = route_of(unit)
        return range(1, reach(sizes, order[stage])) if stage < len(order) else ()

    def keep(unit):
        return pltpu.make_async_copy(own(unit, me), region(unit, me, ()), own_sem.at[unit])

    def start(number, stage):
        for unit in units_in[number]:
            if stage == 0:
                keep(unit).wait()
            for step in steps(unit, stage):
                copy(unit, stage, step, False).start()

    def pass_on(number, stage):
        for unit in units_in[number]:
            for step in steps(unit, stage):
                copy(unit, stage, step, True).wait_recv()
            if stage < 3:
                for step in steps(unit, stage + 1):
                    copy(unit, stage + 1, step, False).start()

    def turn(now):
        if now + AHEAD < total:
            start(now + AHEAD, 0)
        for stage in range(4):
            number = now - GATHER_LAG * stage
            if 0 <= number < total:
                pass_on(number, stage)

    def write(number):
        which, part, tall, wide = chunks[number]
        return pltpu.make_async_copy(
            here[which].at[part], whole[which].at[part], whole_sem.at[number]
        )

    def weight(number, step=None, tile=256):
        which, part, tall, wide = chunks[number]
        if step is None:
            return here[which][part].reshape(-1, wide)
        return here[which][part, :, :, :, :, :, lane_tile(step, tile)].reshape(-1, tile)

    def row_of(name):
        return NARROW.index(name)

    def project(number, left, into, bias=None, plus=None):
        wide = chunks[number][3]

        def body(step, carry):
            columns = lane_tile(step, 256)
            result = product(left[...], weight(number, step))
            if bias is not None:
                result = result + vector[pl.ds(row_of(bias), 1), columns]
            if plus is not None:
                result = result + plus[:, columns].astype(jnp.float32)
            into[:, columns] = result.astype(into.dtype)
            return carry

        tiles(wide // 256, body)

    def save(*names):
        for name in names:
            number = saved.index(name)
            pltpu.make_async_copy(held[name], kept[number], kept_sem.at[number]).start()

    def norm(summed, gain, shift, into, low):
        def body(step, carry):
            lines = pl.ds(pl.multiple_of(step * 64, 64), 64)
            result = normal(
                summed[lines, :],
                vector[pl.ds(row_of(gain), 1), :],
                vector[pl.ds(row_of(shift), 1), :],
            )
            if into is not None:
                into[lines, :] = result
                low[lines, :] = result.astype(low.dtype)
            else:
                low[lines, :] = (result * valid[lines, :]).astype(low.dtype)
            return carry

        lax.fori_loop(0, summed.shape[0] // 64, body, 0)

    def unpack():
        spots = []
        for index in range(devices):
            x = index % side
            c = index // side % cores
            y = index // (side * cores) % near
            spots.append((index // (side * cores * near), y, c, x))
        blocks = [vectors[spot].astype(jnp.float32) for spot in spots]

        def joined(number, fits):
            return sum(blocks[number * fits + 1 : (number + 1) * fits], blocks[number * fits])

        fits = devices * 128 // vector.shape[1]
        for number in range(devices // fits):
            vector[:, pl.ds(128 * number, 128)] = joined(number, fits)
        row = row_of(BUCKET_B)
        fits = devices * 128 // relative.shape[1]
        for number in range(devices // fits):
            vector[pl.ds(row, 1), pl.ds(128 * number, 128)] = joined(number, fits)[row : row + 1]
        row = row_of(FFN_INB)
        for number in range(far * near):
            spot = (number // near, number % near, me[2], me[3])
            wide_bias[:, pl.ds(128 * number, 128)] = vectors[spot].astype(jnp.float32)[row : row + 1]
        hidden[...] = jnp.where(visible(hidden.shape[0] // 2), 0.0, -1e30)

    def heads(low, high, query, keys, values, probs, mixed, biased):
        lane = lax.broadcasted_iota(jnp.int32, (1, 2 * HEAD_DIM), 1)

        def body(pair, carry):
            columns = lane_tile(pair, 2 * HEAD_DIM)
            one, key, value = query[:, columns], keys[:, columns], values[:, columns]
            reach = keys.shape[0]
            for half in range(2):
                mine = lane // HEAD_DIM == half
                room[half, :, pl.ds(0, reach)] = product_right(
                    jnp.where(mine, one, 0).astype(one.dtype), key
                )
            for half in range(2):
                for line in range(0, one.shape[0], LINES):
                    lines = pl.ds(line, LINES)
                    scores = room[half, lines, pl.ds(0, reach)] * 0.125
                    if biased:
                        fit = 128 // BUCKETS
                        table = relative[lines, lane_tile(pair * 2 // fit, 128)]
                        offset = lax.rem(pair * 2, fit) * BUCKETS + half * BUCKETS
                        found = [
                            jnp.take_along_axis(
                                table, buckets[lines, pl.ds(at, 128)] + offset, axis=1
                            )
                            for at in range(0, reach, 128)
                        ]
                        scores = scores + jnp.concatenate(found, axis=1) + hidden[lines, :]
                    probs[pair, lines, pl.ds(half * reach, reach)] = softmax_rows(scores).astype(
                        jnp.bfloat16
                    )
            results = [
                product(probs[pair, :, pl.ds(half * reach, reach)], value) for half in range(2)
            ]
            mixed[:, columns] = jnp.where(lane < HEAD_DIM, *results).astype(mixed.dtype)
            return carry

        lax.fori_loop(low, high, body, 0)

    def self_heads(low, high):
        heads(
            low, high, held[QUERY], held[KEYS], held[VALUES], held[SELF_P], held[MIXED], True
        )

    def cross_heads(low, high):
        heads(
            low, high, held[PROBE], held[INDEX], held[CONTENT], held[CROSS_P], held[JOINED], False
        )

    def to_item(item, source, target, number):
        return pltpu.make_async_remote_copy(
            src_ref=source,
            dst_ref=target,
            send_sem=pair_send.at[number],
            recv_sem=pair_recv.at[number],
            device_id=device_at(sizes, peer_at(sizes, me, GROUP, item)),
            device_id_type=pl.DeviceIdType.MESH,
        )

    lows = held[SECOND_LOW]

    def share(item):
        if item == DIAGONAL:
            return to_item(OTHER, lows.at[NEXT], lows.at[DIAGONAL], DIAGONAL)
        return to_item(item, lows.at[0], lows.at[item], item)

    def partial(kind, part):
        return to_item(
            NEXT if kind == 2 else OTHER,
            partial_out.at[kind, part],
            partial_in.at[kind, part],
            GROUP + 3 * part + kind,
        )

    amount, width = rows.shape
    def feed(number, item):
        part, tall, wide = chunks[number][1:]
        columns = pl.ds(part * wide, wide)
        room[0, :, pl.ds(0, wide)] = product(lows[item], weight(number))

        def body(step, carry):
            for line in range(2):
                lines = pl.ds(pl.multiple_of(step * 64 + line * 32, 32), 32)
                before = room[0, lines, pl.ds(0, wide)] + wide_bias[:, columns]
                error = 1.0 + lax.erf(before * (0.5**0.5))
                held[ACTIVITY][item, lines, columns] = (0.5 * before * error).astype(jnp.bfloat16)
                slope = 0.5 * error + before * jnp.exp(-0.5 * before * before) * (
                    0.3989422804014327
                )
                held[SLOPE][item, lines, columns] = slope.astype(jnp.bfloat16)
            return carry

        lax.fori_loop(0, amount // 64, body, 0)

    def back(number):
        part, tall, wide = chunks[number][1:]
        columns = pl.ds(part * wide, wide)
        activity = held[ACTIVITY]
        partial_out[0, part] = product(activity[OTHER], weight(number)).astype(jnp.bfloat16)
        partial(0, part).start()
        partial_out[1, part] = product(activity[DIAGONAL], weight(number)).astype(jnp.bfloat16)
        partial(1, part).start()
        first[:, columns] = product(activity[NEXT], weight(number))
        held[SUM_THIRD][:, columns] = (
            product(activity[0], weight(number))
            + vector[pl.ds(row_of(FFN_OUTB), 1), columns]
            + second[:, columns]
        )

    def relay(part):
        wide = width // GROUP
        partial(1, part).wait_recv()
        total_of = first[:, pl.ds(part * wide, wide)] + partial_in[1, part].astype(jnp.float32)
        partial_out[2, part] = total_of.astype(jnp.bfloat16)
        partial(2, part).start()

    pairs = held[QUERY].shape[1] // (2 * HEAD_DIM)

    def compute(number):
        which, part, tall, wide = chunks[number]
        if which < 0:
            unpack()
            save(VECTOR)
            return
        write(number).start()
        name = MATRICES[which]
        if name == SELF_Q:
            project(number, rows, held[QUERY], SELF_QB)
            save(QUERY)
        elif name == SELF_K:
            project(number, rows, held[KEYS])
            save(KEYS)
        elif name == SELF_V:
            project(number, rows, held[VALUES], SELF_VB)
            save(VALUES)
        elif name == BUCKET_W:
            project(number, rows, relative, BUCKET_B)
            self_heads(0, pairs // 2)
        elif name == SELF_O:
            self_heads(pairs // 2, pairs)
            save(SELF_P, MIXED)
            project(number, held[MIXED], held[SUM_FIRST], SELF_OB, rows)
            save(SUM_FIRST)
            norm(held[SUM_FIRST], GAIN_A, SHIFT_A, first, held[FIRST_LOW])
            save(FIRST_LOW)
        elif name == CROSS_K:
            project(number, enc, held[INDEX])
            save(INDEX)
        elif name == CROSS_V:
            project(number, enc, held[CONTENT], CROSS_VB)
            save(CONTENT)
            cross_heads(0, pairs // 2)
        elif name == CROSS_Q:
            project(number, held[FIRST_LOW], held[PROBE], CROSS_QB)
            save(PROBE)
        elif name == CROSS_O:
            cross_heads(pairs // 2, pairs)
            save(CROSS_P, JOINED)
            project(number, held[JOINED], held[SUM_SECOND], CROSS_OB, first)
            save(SUM_SECOND)
            norm(held[SUM_SECOND], GAIN_B, SHIFT_B, second, lows.at[0])
            share(NEXT).start()
            share(OTHER).start()
        elif name == FFN_IN:
            feed(number, 0)
            if part == 2:
                share(OTHER).wait_recv()
                for earlier in (number - 2, number - 1):
                    feed(earlier, OTHER)
                share(NEXT).wait_recv()
                share(DIAGONAL).start()
                for earlier in (number - 2, number - 1):
                    feed(earlier, NEXT)
                share(DIAGONAL).wait_recv()
                for earlier in (number - 2, number - 1):
                    feed(earlier, DIAGONAL)
                save(SECOND_LOW)
            if part >= 2:
                for item in (OTHER, NEXT, DIAGONAL):
                    feed(number, item)
            if part == 3:
                save(SLOPE, ACTIVITY)
        elif name == FFN_OUT:
            back(number)
            if part > 0:
                relay(part - 1)

    for unit in range(len(units)):
        keep(unit).start()
    enter(sizes, me)
    for number in range(min(AHEAD, total)):
        start(number, 0)
    done = 0
    for now in range(total + 3 * GATHER_LAG):
        turn(now)
        while done < total and (
            done + GATHER_LAG * (len(gather_route(chunks[done][0], 0)) - 1) <= now
        ):
            compute(done)
            done += 1
    relay(GROUP - 1)
    wide = width // GROUP
    for part in range(GROUP):
        partial(0, part).wait_recv()
        partial(2, part).wait_recv()
        held[SUM_THIRD][:, pl.ds(part * wide, wide)] += partial_in[0, part].astype(
            jnp.float32
        ) + partial_in[2, part].astype(jnp.float32)
    save(SUM_THIRD)
    norm(held[SUM_THIRD], GAIN_C, SHIFT_C, None, outputs)
    for unit in range(len(units)):
        for stage in range(4):
            for step in steps(unit, stage):
                copy(unit, stage, step, False).wait_send()
    for item in (NEXT, OTHER, DIAGONAL):
        share(item).wait_send()
    for part in range(GROUP):
        for kind in range(3):
            partial(kind, part).wait_send()
    for number in range(1, total):
        write(number).wait()
    for number, name in enumerate(saved):
        pltpu.make_async_copy(held[name], kept[number], kept_sem.at[number]).wait()


def forward_all(sizes, small, blocks, rows, enc, buckets, valid):
    devices = sizes[0] * sizes[1] * sizes[2] * sizes[3]
    chunks = [(-1, 0, False, 128)]
    shapes = []
    units = 1
    for which, block in enumerate(blocks):
        part, parts = parts_of(devices, which, block.shape)
        shape = tuple(sizes[level] for level in levels_of(which))
        shapes.append(jax.ShapeDtypeStruct((parts,) + shape + part, block.dtype))
    done = dict.fromkeys(MATRICES, 0)
    for which in GATHER_ORDER:
        part = shapes[which].shape[-2:]
        units += len(units_of(which, *part))
        chunks.append((which, done[which], part[0] > ROWS, part[1]))
        done[which] += 1
    amount, width = rows.shape
    source = enc.shape[0]
    hidden_units = blocks[MATRICES.index(FFN_IN)].shape[-1]
    buckets_wide = blocks[MATRICES.index(BUCKET_W)].shape[1]
    head_count = width // HEAD_DIM
    low, full = jnp.bfloat16, jnp.float32
    one, two = (amount, width), (source, width)
    saved = {
        QUERY: (one, low), KEYS: (one, low), VALUES: (one, low), MIXED: (one, low),
        FIRST_LOW: (one, low), PROBE: (one, low), JOINED: (one, low),
        SECOND_LOW: ((GROUP,) + one, low), INDEX: (two, low), CONTENT: (two, low),
        SUM_FIRST: (one, full), SUM_SECOND: (one, full), SUM_THIRD: (one, full),
        SLOPE: ((GROUP, amount, hidden_units), low), ACTIVITY: ((GROUP, amount, hidden_units), low),
        SELF_P: ((head_count // 2, amount, 2 * amount), low),
        CROSS_P: ((head_count // 2, amount, 2 * source), low),
        VECTOR: ((16, width), full),
    }
    names = SAVED
    unused, places = slots(sizes)
    any_spec = pl.BlockSpec(memory_space=pl.ANY)
    vmem_spec = pl.BlockSpec(memory_space=pltpu.VMEM)
    held = [pltpu.VMEM(*saved[name]) for name in names]
    results = pl.pallas_call(
        partial(forward_kernel, sizes, chunks, names),
        out_shape=[jax.ShapeDtypeStruct(one, low)]
        + shapes
        + [jax.ShapeDtypeStruct(*saved[name]) for name in names],
        in_specs=[vmem_spec] * 4 + [any_spec] * (1 + len(blocks)),
        out_specs=[vmem_spec] + [any_spec] * (len(shapes) + len(names)),
        scratch_shapes=held
        + [pltpu.VMEM(entry.shape, entry.dtype) for entry in shapes]
        + [
            pltpu.VMEM(sizes + small.shape, low),
            pltpu.VMEM((amount, buckets_wide), full),
            pltpu.VMEM((amount, amount), full),
            pltpu.VMEM(one, full),
            pltpu.VMEM(one, full),
            pltpu.VMEM((1, hidden_units), full),
            pltpu.VMEM((3, GROUP, amount, width // GROUP), low),
            pltpu.VMEM((3, GROUP, amount, width // GROUP), low),
            pltpu.VMEM((2, amount, max(amount, source)), full),
            pltpu.SemaphoreType.DMA((len(names),)),
            pltpu.SemaphoreType.DMA((len(chunks),)),
            pltpu.SemaphoreType.DMA((4 * GROUP,)),
            pltpu.SemaphoreType.DMA((4 * GROUP,)),
            pltpu.SemaphoreType.DMA((units,)),
            pltpu.SemaphoreType.DMA((units, places)),
            pltpu.SemaphoreType.DMA((units, places)),
        ],
        compiler_params=pltpu.CompilerParams(
            collective_id=0, has_side_effects=True, vmem_limit_bytes=63 * 1024 * 1024
        ),
        cost_estimate=pl.CostEstimate(flops=10**10, bytes_accessed=1 << 27, transcendentals=10**7),
        name="forward_all",
    )(rows, enc, buckets, valid, small, *blocks)
    whole = dict(zip(MATRICES, results[1 : 1 + len(blocks)]))
    return results[0], whole, dict(zip(names, results[1 + len(blocks) :]))


def backward_kernel(sizes, chunks, flat_room, *refs):
    far, near, cores, side = sizes
    devices = far * near * cores * side
    count = len(MATRICES)
    cotangent, buckets, valid, rows_in, enc_in = refs[:5]
    kept, refs = refs[5 : 5 + len(SAVED)], refs[5 + len(SAVED) :]
    whole, refs = refs[:count], refs[count:]
    small_out, shares, refs = refs[0], refs[1 : 1 + count], refs[1 + count :]
    tokens_out, encoded_out, refs = refs[0], refs[1], refs[2:]
    pool, full, acc, vector, sums, wide_sums, small, relative, picked, room, steep = refs[:11]
    low_slot, tall_slot, self_probs, cross_probs, flat_ring, tall_ring, flat_in = refs[11:18]
    refs = refs[18:]
    total = len(chunks) + 1
    units = []
    units_in = []
    inbox = []
    flats = []
    for number in range(total):
        if number < total - 1:
            which, tall_rows, tall, wide, column = chunks[number]
            own_units = units_of(which, tall_rows, wide)
            if which not in (FFN_IN, FFN_OUT):
                flats.append(number)
        else:
            which = -1
            own_units = units_of(which, *small.shape[4:])
        units_in.append(range(len(units), len(units) + len(own_units)))
        for unit in own_units:
            units.append((number,) + unit)
            if flats and flats[-1] == number:
                shelf = flat_in.at[pl.ds((len(flats) - 1) % flat_room, 1)]
                shelf = shelf.at[:, :, :, :, :, pl.ds(unit[2], unit[3])]
                inbox.append((shelf,) + tuple(refs[:3]))
                refs = refs[3:]
            else:
                deep = len(sum_route(which, 0))
                inbox.append(tuple(refs[:deep]))
                refs = refs[deep:]
    load_sem, slot_sem, self_sem, cross_sem, out_sem, credit = refs[:6]
    pair_send, pair_recv, send_sem, recv_sem = refs[6:]
    me = place(sizes)
    first, unused = slots(sizes)
    z, y, c, x = me
    amount, width = rows_in.shape
    source = enc_in.shape[0]
    pairs = width // (2 * HEAD_DIM)
    slab = width // far

    def loading(which, number, height=1):
        array = {RB: rows_in, EB: enc_in, CB: cotangent}.get(which)
        array = kept[which] if array is None else array
        if which in (SUM_FIRST, SUM_SECOND, SUM_THIRD):
            return [(array, full.at[number], which)]
        if which == VECTOR:
            return [(array, vector, which)]
        if height == 1:
            return [(array, pool.at[number], which)]
        if len(array.shape) == 3:
            return [
                (
                    array.at[part],
                    pool.at[number + part],
                    which,
                )
                for part in range(height)
            ]
        return [
            (array.at[pl.ds(part * amount, amount)], pool.at[number + part], which)
            for part in range(height)
        ]

    semaphores = {}
    waiting = {}

    def fetch(which, number, height=1):
        waiting[which] = []
        for source_ref, target, unused_name in loading(which, number, height):
            semaphores[which, len(waiting[which])] = len(semaphores)
            one = pltpu.make_async_copy(source_ref, target, load_sem.at[len(semaphores) - 1])
            one.start()
            waiting[which].append(one)

    def ready(*names):
        for which in names:
            for one in waiting.pop(which):
                one.wait()

    order = [FFN_IN, CROSS_O, CROSS_Q, SELF_O, CROSS_K, CROSS_V, SELF_Q, SELF_K, SELF_V, BUCKET_W]

    def weight_copies(number):
        which = order[number]
        parts, wide = whole[which].shape[0], whole[which].shape[-1]
        return [
            pltpu.make_async_copy(
                whole[which].at[part],
                low_slot.at[number % 2, :, :, :, :, :, pl.ds(part * wide, wide)],
                slot_sem.at[number % 2 * GROUP + part],
            )
            for part in range(parts)
        ]

    def weight_fetch(number):
        if number < len(order):
            for one in weight_copies(number):
                one.start()

    def weight_ready(number):
        for one in weight_copies(number):
            one.wait()

    def tall_copy():
        return pltpu.make_async_copy(whole[FFN_OUT], tall_slot, slot_sem.at[2 * GROUP])

    def row_of(name):
        return NARROW.index(name)

    def through(which, left, into, fresh=False):
        number = order.index(which)
        wide = whole[which].shape[0] * whole[which].shape[-1]

        def body(step, carry):
            columns = lane_tile(step, slab)
            piece = low_slot[number % 2, step, :, :, :, :, pl.ds(0, wide)].reshape(slab, wide)
            result = product_right(left(), piece)
            if fresh:
                into[:, columns] = result.astype(into.dtype)
            else:
                into[:, columns] += result
            return carry

        tiles(far, body)

    def back_through(which, left, into, fresh=False):
        weight_ready(order.index(which))
        through(which, left, into, fresh)
        weight_fetch(order.index(which) + 2)

    def norm_backward(summed, gain, shift, bias, low, first_grad):
        def body(step, carry):
            lines = pl.ds(pl.multiple_of(step * 64, 64), 64)
            center = summed[lines, :]
            center = center - jnp.mean(center, axis=-1, keepdims=True)
            scale = lax.rsqrt(jnp.mean(center * center, axis=-1, keepdims=True) + 1e-05)
            unit = center * scale
            if first_grad is not None:
                grad = first_grad[lines, :].astype(jnp.float32) * valid[lines, :]
            else:
                grad = acc[lines, :]
            inner = grad * vector[pl.ds(row_of(gain), 1), :]
            inner = inner - jnp.mean(inner, axis=-1, keepdims=True) - unit * jnp.mean(
                inner * unit, axis=-1, keepdims=True
            )
            inner = inner * scale
            branch = inner.astype(jnp.bfloat16)
            acc[lines, :] = inner
            low[lines, :] = branch
            sums[pl.ds(row_of(gain), 1), :] += jnp.sum(grad * unit, axis=0, keepdims=True)
            sums[pl.ds(row_of(shift), 1), :] += jnp.sum(grad, axis=0, keepdims=True)
            sums[pl.ds(row_of(bias), 1), :] += jnp.sum(
                branch.astype(jnp.float32), axis=0, keepdims=True
            )
            return carry

        lax.fori_loop(0, amount // 64, body, 0)

    def feed_backward(item):
        parts, wide = whole[FFN_OUT].shape[0], whole[FFN_OUT].shape[-1]
        tile = near * chunks[0][1]

        def body(step, carry):
            columns = lane_tile(step, tile)
            grad = 0.0
            for part in range(parts):
                piece = tall_slot[part, step].reshape(tile, wide)
                left = pool[BRANCH_THREE + item, :, pl.ds(part * wide, wide)]
                grad = grad + product_right(left, piece)
            slope = pool[SLOPES + item, :, columns].astype(jnp.float32)
            grad = (grad * slope).astype(jnp.bfloat16)
            pool[SLOPES + item, :, columns] = grad
            wide_sums[:, columns] += jnp.sum(grad.astype(jnp.float32), axis=0, keepdims=True)
            return carry

        tiles(far, body)

    def probs_copy(which, pair, slot):
        buffer, sem = (cross_probs, cross_sem) if which == CROSS_P else (self_probs, self_sem)
        return pltpu.make_async_copy(kept[which].at[pair], buffer.at[slot], sem.at[slot])

    def heads_backward(which, low, high, places, tall):
        query, keys, values, grad_out, to_query, to_keys, to_values = places
        buffer = cross_probs if which == CROSS_P else self_probs
        lane = lax.broadcasted_iota(jnp.int32, (1, 2 * HEAD_DIM), 1)
        span = tall * amount

        def body(pair, carry):
            columns = lane_tile(pair, 2 * HEAD_DIM)
            slot = lax.rem(pair, 2)
            probs_copy(which, pair, slot).wait()

            @pl.when(pair + 1 < pairs)
            def _():
                probs_copy(which, pair + 1, 1 - slot).start()

            one = pool[query, :, columns]
            grad = pool[grad_out, :, columns]
            key = pool[pl.ds(keys, tall), :, columns].reshape(span, 2 * HEAD_DIM)
            value = pool[pl.ds(values, tall), :, columns].reshape(span, 2 * HEAD_DIM)
            found = []
            for half in range(2):
                mine = lane // HEAD_DIM == half
                room[half, :, pl.ds(0, span)] = product_right(
                    jnp.where(mine, grad, 0).astype(grad.dtype), value
                )
            for half in range(2):
                for line in range(0, amount, LINES):
                    lines = pl.ds(line, LINES)
                    prob = buffer[slot, lines, pl.ds(half * span, span)].astype(jnp.float32)
                    weighted = prob * room[half, lines, pl.ds(0, span)]
                    scores = weighted - prob * jnp.sum(weighted, axis=-1, keepdims=True)
                    scores = scores.astype(jnp.bfloat16)
                    steep[half, lines, pl.ds(0, span)] = scores
                    if which == SELF_P:
                        picked[half, lines, :] = scores[:, :target].astype(jnp.float32)
                if which == SELF_P:
                    gather_buckets(pair, half)
            for half in range(2):
                scores = steep[half, :, pl.ds(0, span)]
                prob = buffer[slot, :, pl.ds(half * span, span)]
                found.append(
                    (
                        product(scores, key) * 0.125,
                        product_left(scores, one) * 0.125,
                        product_left(prob, grad),
                    )
                )
            if which == SELF_P:
                spread_buckets(pair)
            merged = [
                jnp.where(lane < HEAD_DIM, left, right).astype(jnp.bfloat16)
                for left, right in zip(*found)
            ]
            pool[to_query, :, columns] = merged[0]
            pool[pl.ds(to_keys, tall), :, columns] = merged[1].reshape(tall, amount, 2 * HEAD_DIM)
            pool[pl.ds(to_values, tall), :, columns] = merged[2].reshape(tall, amount, 2 * HEAD_DIM)
            biases = (SELF_QB, SELF_VB) if which == SELF_P else (CROSS_QB, CROSS_VB)
            for bias, grads in zip(biases, (merged[0], merged[2])):
                sums[pl.ds(row_of(bias), 1), columns] = jnp.sum(
                    grads.astype(jnp.float32), axis=0, keepdims=True
                )
            return carry

        lax.fori_loop(low, high, body, 0)

    target = amount // 2
    fit = 128 // BUCKETS

    def gather_buckets(pair, half):
        own = steep[half, pl.ds(target, target), pl.ds(target, target)].astype(jnp.float32)
        own = jnp.sum(own, axis=1, keepdims=True)
        line = lax.broadcasted_iota(jnp.int32, (target, target), 0)
        lane = lax.broadcasted_iota(jnp.int32, (target, target), 1)
        bucket = jnp.sum(
            jnp.where(line == lane, buckets[target:, target:], 0).astype(jnp.float32),
            axis=1,
            keepdims=True,
        ).astype(jnp.int32)
        offset = lax.rem(pair * 2, fit) * BUCKETS + half * BUCKETS
        block = lane_tile(pair * 2 // fit, 128)
        relative[pl.ds(target, target), block] += jnp.where(lane == bucket + offset, own, 0.0)

    def spread_buckets(pair):
        block = lane_tile(pair * 2 // fit, 128)
        some = 8
        line = lax.broadcasted_iota(jnp.int32, (some * target, 128), 0)
        lane = lax.broadcasted_iota(jnp.int32, (some * target, 128), 1)

        def body(step, carry):
            for half in range(2):
                offset = lax.rem(pair * 2, fit) * BUCKETS + half * BUCKETS
                held = [
                    jnp.where(
                        buckets[:, :target] == some * step + other, picked[half], 0.0
                    ).astype(jnp.bfloat16)
                    for other in range(some)
                ]
                chosen = lane == offset + some * step + line // target
                relative[:, block] += product(
                    jnp.concatenate(held, axis=1), jnp.where(chosen, 1.0, 0.0).astype(jnp.bfloat16)
                )
            return carry

        lax.fori_loop(0, BUCKETS // some, body, 0)

    def held(number):
        if number == total - 1:
            return small, None
        tall, wide = chunks[number][2:4]
        same = [other for other in range(number) if chunks[other][2] == tall]
        ring = tall_ring if tall else flat_ring
        size = ring.shape[0]
        ref = ring.at[len(same) % size]
        if not tall:
            ref = ref.at[:, :, :, :, :, pl.ds(0, wide)]
        return ref, same[-size] if len(same) >= size else None

    def stage_of(unit, stage):
        number, row, tall_rows, column, columns, route = units[unit]
        which = chunks[number][0] if number < total - 1 else -1
        order_of = sum_route(which, route)
        before = without(levels_of(which), order_of[:stage])
        if stage == 0:
            from_ref = held(number)[0]
            if number < total - 1:
                every = (slice(None),) * len(levels_of(which))
                from_ref = from_ref.at[every + (pl.ds(row, tall_rows), pl.ds(column, columns))]
        else:
            from_ref = inbox[unit][stage - 1].at[0]
        return from_ref, before, order_of[stage], inbox[unit][stage]

    def pick(ref, levels, level, spot, step=None):
        index = []
        for other in levels:
            if other == level or (level == GROUP and other in (2, 3)):
                index.append(spot[other])
            elif other == 0 and step is not None:
                index.append(step)
            else:
                index.append(slice(None))
        return ref.at[tuple(index)] if index else ref

    def stages(unit):
        number = units[unit][0]
        return len(sum_route(chunks[number][0] if number < total - 1 else -1, 0))

    def copies(unit, stage):
        if stage >= stages(unit):
            return []
        from_ref, before, level, into = stage_of(unit, stage)
        found = []
        for step in range(1, reach(sizes, level)):
            peer = peer_at(sizes, me, level, step)
            slot = first[level] + step - 1
            found.append(
                pltpu.make_async_remote_copy(
                    src_ref=pick(from_ref, before, level, peer),
                    dst_ref=into.at[step - 1],
                    send_sem=send_sem.at[unit, slot],
                    recv_sem=recv_sem.at[unit, slot],
                    device_id=device_at(sizes, peer),
                    device_id_type=pl.DeviceIdType.MESH,
                )
            )
        return found

    def start(number):
        if number in flats and flats.index(number) >= flat_room:
            pl.semaphore_wait(credit, cores - 1)
        for unit in units_in[number]:
            for one in copies(unit, 0):
                one.start()

    waited = set()

    def sent(number, stage):
        for unit in units_in[number]:
            if (unit, stage) not in waited:
                waited.add((unit, stage))
                for one in copies(unit, stage):
                    one.wait_send()

    def add(unit, stage):
        if stage >= stages(unit):
            return
        from_ref, before, level, into = stage_of(unit, stage)
        after = without(before, (level,))
        number, row, tall_rows, column, columns, route = units[unit]
        last = stage == stages(unit) - 1
        if last and number < total - 1 and chunks[number][0] == FFN_IN:
            spot = (pl.ds(row, tall_rows), pl.ds(chunks[number][4] + column, columns))
            shares[FFN_IN][(number_in_group(sizes, me),) + spot] = from_ref[c, x].astype(jnp.float32)
            for step in range(1, reach(sizes, GROUP)):
                peer = peer_at(sizes, me, GROUP, step)
                shares[FFN_IN][(number_in_group(sizes, peer),) + spot] = into[step - 1].astype(
                    jnp.float32
                )
            return

        def one(step):
            here = pick(from_ref, before, level, me, step)[...]
            if last:
                here = here.astype(jnp.float32)
            for other in range(1, reach(sizes, level)):
                here = here + pick(into.at[other - 1], after, None, None, step)[...]
            return here

        if last:
            if number == total - 1:
                small_out[...] = one(None)
            else:
                which, block_rows, tall, wide, base = chunks[number]
                shares[which][pl.ds(row, tall_rows), pl.ds(base + column, columns)] = one(None)
        elif 0 in after:

            def body(step, carry):
                pick(into.at[0], after, None, None, step)[...] = one(step)
                return carry

            lax.fori_loop(0, far, body, 0)
        else:
            into[0] = one(None)

    def pass_on(number, stage):
        for unit in units_in[number]:
            for one in copies(unit, stage):
                one.wait_recv()
            add(unit, stage)
            if stage < 3:
                for one in copies(unit, stage + 1):
                    one.start()
        if stage == 1 and number in flats and flats.index(number) + flat_room < len(flats):
            sent(number, 1)
            for step in range(1, cores):
                pl.semaphore_signal(
                    credit,
                    inc=1,
                    device_id=device_at(sizes, moved(me, 2, lax.rem(c + step, cores))),
                    device_id_type=pl.DeviceIdType.MESH,
                )

    def produce(number, left, right):
        ref, previous = held(number)
        if previous is not None:
            sent(previous, 0)
        which, tall_rows, tall, wide, column = chunks[number]
        height = near * tall_rows if tall else slab
        right_value = right

        def body(step, carry):
            grad = product_left(left(step, height), right_value()).astype(jnp.bfloat16)
            into = ref.at[step]
            into[...] = grad.reshape(into.shape)
            return carry

        tiles(far, body)

    emitted = {}

    def emit(now, number, left=None, right=None):
        if left is not None:
            produce(number, left, right)
        start(number)
        emitted[number] = now

    def turn(now):
        for stage in (3, 2, 1, 0):
            for number, began in emitted.items():
                if began + 1 + LAG * stage == now:
                    pass_on(number, stage)

    def lanes_of(slot, height=1):
        def part(step, wide):
            if height == 1:
                return pool[slot, :, lane_tile(step, wide)]
            return pool[pl.ds(slot, height), :, lane_tile(step, wide)].reshape(height * amount, wide)

        return part

    def all_of(slot, height=1, wide=None):
        wide = width if wide is None else wide

        def part():
            if height == 1:
                return pool[slot, :, pl.ds(0, wide)]
            return pool[pl.ds(slot, height), :, pl.ds(0, wide)].reshape(height * amount, wide)

        return part

    fetch(SUM_THIRD, 0)
    fetch(CB, COTANGENT)
    fetch(VECTOR, 0)
    tall_copy().start()
    fetch(SLOPE, SLOPES, GROUP)
    weight_fetch(0)
    weight_fetch(1)
    fetch(ACTIVITY, ACTIVITIES, GROUP)
    fetch(SECOND_LOW, SECONDS, GROUP)
    wide_sums[...] = jnp.zeros_like(wide_sums)
    fetch(SUM_SECOND, 1)
    fetch(JOINED, JOINEDS)
    fetch(PROBE, PROBES)
    fetch(INDEX, INDEXES, 2)
    fetch(CONTENT, CONTENTS, 2)
    fetch(FIRST_LOW, FIRSTS)
    probs_copy(CROSS_P, 0, 0).start()
    probs_copy(SELF_P, 0, 0).start()
    sums[...] = jnp.zeros_like(sums)
    relative[...] = jnp.zeros_like(relative)
    enter(sizes, me)

    ready(SUM_THIRD, CB, VECTOR)
    norm_backward(full.at[0], GAIN_C, SHIFT_C, FFN_OUTB, pool.at[BRANCH_THREE], pool.at[COTANGENT])

    def to_item(item, source_slot, target_slot, number):
        return pltpu.make_async_remote_copy(
            src_ref=pool.at[source_slot],
            dst_ref=pool.at[target_slot],
            send_sem=pair_send.at[number],
            recv_sem=pair_recv.at[number],
            device_id=device_at(sizes, peer_at(sizes, me, GROUP, item)),
            device_id_type=pl.DeviceIdType.MESH,
        )

    branch_next = to_item(NEXT, BRANCH_THREE, BRANCH_THREE + NEXT, 0)
    branch_other = to_item(OTHER, BRANCH_THREE, BRANCH_THREE + OTHER, 1)
    branch_diagonal = to_item(OTHER, BRANCH_THREE + NEXT, BRANCH_THREE + DIAGONAL, 2)
    partial_other = to_item(OTHER, PARTIALS + OTHER, PARTIAL_OTHER, 3)
    partial_diagonal = to_item(OTHER, PARTIALS + DIAGONAL, PARTIAL_DIAGONAL, 4)
    partial_next = to_item(NEXT, PARTIALS + NEXT, PARTIAL_NEXT, 5)

    def slab_backward(item):
        feed_backward(item)
        left = all_of(SLOPES + item)
        if item == 0:
            through(FFN_IN, left, acc)
        else:
            through(FFN_IN, left, pool.at[PARTIALS + item], True)

    branch_next.start()
    branch_other.start()
    tall_copy().wait()
    ready(SLOPE)
    weight_ready(0)
    slab_backward(0)
    branch_other.wait()
    slab_backward(OTHER)
    partial_other.start()
    branch_next.wait_recv()
    branch_diagonal.start()
    ready(ACTIVITY, SECOND_LOW)
    fetch(SUM_FIRST, 0)

    def activity_lanes(step, wide):
        columns = lane_tile(step, wide)
        return pool[pl.ds(ACTIVITIES, GROUP), :, columns].reshape(GROUP * amount, wide)

    def third_lanes(part):
        wide = chunks[part][3]
        return lambda: pool[pl.ds(BRANCH_THREE, GROUP), :, pl.ds(part * wide, wide)].reshape(
            GROUP * amount, wide
        )

    def slab_lanes(part):
        wide = chunks[GROUP + part][3]
        return lambda: pool[pl.ds(SLOPES, GROUP), :, pl.ds(part * wide, wide)].reshape(
            GROUP * amount, wide
        )

    cross_places = (PROBES, INDEXES, CONTENTS, GRAD_JOINED, GRAD_PROBE, GRAD_INDEX, GRAD_CONTENT)
    self_places = (QUERIES, KEYSES, VALUESES, GRAD_MIXED, GRAD_QUERY, GRAD_KEYS, GRAD_VALUES)

    def second_backward():
        ready(SUM_SECOND, JOINED, PROBE, INDEX, CONTENT, FIRST_LOW)
        partial_other.wait()
        partial_next.wait()
        acc[...] += pool[PARTIAL_OTHER].astype(jnp.float32) + pool[PARTIAL_NEXT].astype(jnp.float32)
        norm_backward(full.at[1], GAIN_B, SHIFT_B, CROSS_OB, pool.at[BRANCH_TWO], None)
        back_through(CROSS_O, all_of(BRANCH_TWO), pool.at[GRAD_JOINED], True)

    def cross_backward(low):
        heads_backward(CROSS_P, low, low + pairs // 4, cross_places, source // amount)

    def first_backward():
        back_through(CROSS_Q, all_of(GRAD_PROBE), acc)
        ready(SUM_FIRST)
        norm_backward(full.at[0], GAIN_A, SHIFT_A, SELF_OB, pool.at[BRANCH_ONE], None)
        back_through(SELF_O, all_of(BRANCH_ONE), pool.at[GRAD_MIXED], True)

    def self_backward(low):
        if low == 0:
            ready(QUERY, KEYS, VALUES)
        heads_backward(SELF_P, low, low + pairs // 4, self_places, 1)

    step = pairs // 4
    slab_backward(NEXT)
    branch_diagonal.wait_recv()
    emit(0, 0, activity_lanes, third_lanes(0))
    slab_backward(DIAGONAL)
    weight_fetch(2)
    partial_diagonal.start()
    turn(0)
    emit(1, 1, activity_lanes, third_lanes(1))
    partial_diagonal.wait_recv()
    pool[PARTIALS + NEXT] = (
        pool[PARTIALS + NEXT].astype(jnp.float32) + pool[PARTIAL_DIAGONAL].astype(jnp.float32)
    ).astype(jnp.bfloat16)
    partial_next.start()
    for one in (branch_next, branch_diagonal, partial_diagonal):
        one.wait_send()
    turn(1)
    emit(2, 2, activity_lanes, third_lanes(2))
    turn(2)
    emit(3, 3, activity_lanes, third_lanes(3))
    turn(3)
    emit(4, 4, lanes_of(SECONDS, GROUP), slab_lanes(0))
    second_backward()
    turn(4)
    emit(5, 5, lanes_of(SECONDS, GROUP), slab_lanes(1))
    cross_backward(0)
    turn(5)
    emit(6, 6, lanes_of(SECONDS, GROUP), slab_lanes(2))
    cross_backward(step)
    turn(6)
    emit(7, 7, lanes_of(SECONDS, GROUP), slab_lanes(3))
    fetch(EB, ENCODED, 2)
    fetch(QUERY, QUERIES)
    fetch(MIXED, MIXEDS)
    cross_backward(2 * step)
    turn(7)
    emit(8, 8, lanes_of(JOINEDS), all_of(BRANCH_TWO))
    fetch(KEYS, KEYSES)
    cross_backward(3 * step)
    fetch(VALUES, VALUESES)
    fetch(RB, TOKENS)
    turn(8)
    emit(9, 9, lanes_of(FIRSTS), all_of(GRAD_PROBE))
    first_backward()
    turn(9)
    ready(EB)
    emit(10, 10, lanes_of(ENCODED, 2), all_of(GRAD_CONTENT, 2))
    self_backward(0)
    turn(10)
    emit(11, 11, lanes_of(ENCODED, 2), all_of(GRAD_INDEX, 2))
    self_backward(step)
    turn(11)
    ready(MIXED)
    emit(12, 12, lanes_of(MIXEDS), all_of(BRANCH_ONE))
    self_backward(2 * step)
    turn(12)
    self_backward(3 * step)
    ready(RB)
    now = 13
    pool[GRAD_RELATIVE, :, pl.ds(0, relative.shape[1])] = relative[...].astype(jnp.bfloat16)
    sums[pl.ds(row_of(BUCKET_B), 1), pl.ds(0, relative.shape[1])] = jnp.sum(
        relative[...].astype(jnp.bfloat16).astype(jnp.float32), axis=0, keepdims=True
    )
    fits = devices * 128 // width
    for index in range(devices):
        spot = (
            index // (side * cores * near),
            index // (side * cores) % near,
            index // side % cores,
            index % side,
        )
        small[spot] = sums[:, pl.ds(index // fits * 128, 128)]
        block = index * relative.shape[1] // (devices * 128)
        small[spot + (pl.ds(row_of(BUCKET_B), 1),)] = sums[
            pl.ds(row_of(BUCKET_B), 1), pl.ds(block * 128, 128)
        ]
    for index in range(far * near):
        spot = (index // near, index % near, c, x)
        small[spot + (pl.ds(row_of(FFN_INB), 1),)] = wide_sums[:, pl.ds(index * 128, 128)]
    emit(now, 17)
    last = (
        (13, GRAD_VALUES, width),
        (14, GRAD_KEYS, width),
        (15, GRAD_QUERY, width),
        (16, GRAD_RELATIVE, relative.shape[1]),
    )
    for number, grads, wide in last:
        emit(now, number, lanes_of(TOKENS), all_of(grads, 1, wide))
        turn(now)
        now += 1

    def encoded_part(which, slot, fresh):
        number = order.index(which)
        weight_ready(number)

        def body(step, carry):
            columns = lane_tile(step, slab)
            piece = low_slot[number % 2, step].reshape(slab, width)
            result = product_right(all_of(slot, 2)(), piece)
            for part in range(source // amount):
                lines = result[part * amount : (part + 1) * amount]
                if fresh:
                    full[part, :, columns] = lines
                else:
                    full[part, :, columns] += lines
            return carry

        tiles(far, body)
        weight_fetch(number + 2)

    drain = [
        lambda: encoded_part(CROSS_K, GRAD_INDEX, True),
        lambda: encoded_part(CROSS_V, GRAD_CONTENT, False),
        lambda: back_through(SELF_Q, all_of(GRAD_QUERY), acc),
        lambda: back_through(SELF_K, all_of(GRAD_KEYS), acc),
        lambda: back_through(SELF_V, all_of(GRAD_VALUES), acc),
        lambda: back_through(BUCKET_W, all_of(GRAD_RELATIVE, 1, relative.shape[1]), acc),
    ]
    results = [
        pltpu.make_async_copy(
            full.at[part], encoded_out.at[pl.ds(part * amount, amount)], out_sem.at[part]
        )
        for part in range(source // amount)
    ]
    results.append(pltpu.make_async_copy(acc, tokens_out, out_sem.at[len(results)]))
    end = max(emitted.values()) + 1 + 3 * LAG
    piece = 0
    while now <= end or piece < len(drain):
        if piece < len(drain):
            drain[piece]()
            piece += 1
            if piece == 2:
                for one in results[:-1]:
                    one.start()
            if piece == len(drain):
                results[-1].start()
        turn(now)
        now += 1
    for number in range(total):
        for stage in range(4):
            sent(number, stage)
    for one in results:
        one.wait()


def backward_all(sizes, whole, kept, rows, enc, cotangent, buckets, valid):
    devices = sizes[0] * sizes[1] * sizes[2] * sizes[3]
    chunks = []
    for which in SUM_ORDER:
        parts, tall_rows, wide = whole[which].shape[0], whole[which].shape[-2], whole[which].shape[-1]
        for part in range(parts):
            chunks.append((which, tall_rows, tall_rows > ROWS, wide, part * wide))
    flat_room, low, full = 6, jnp.bfloat16, jnp.float32
    amount, width = rows.shape
    wide_rows, tall_wide = whole[FFN_OUT].shape[-2:]
    hidden_units = wide_rows * devices // GROUP
    buckets_wide = whole[BUCKET_W].shape[-1]
    far, near, cores, side = sizes
    inbox = []
    total = 0
    for number in range(len(chunks) + 1):
        summed = number < len(chunks)
        block = (chunks[number][1], chunks[number][3]) if summed else (16, 128)
        kind = low if summed else full
        which = chunks[number][0] if summed else -1
        for row, tall_rows, column, columns, route in units_of(which, *block):
            total += 1
            left = levels_of(which)
            for stage, level in enumerate(sum_route(which, route)):
                left = without(left, (level,))
                if stage > 0 or which in (FFN_IN, FFN_OUT, -1):
                    shape = (reach(sizes, level) - 1,) + tuple(sizes[one] for one in left)
                    inbox.append(pltpu.VMEM(shape + (tall_rows, columns), kind))
    unused, places = slots(sizes)
    any_spec = pl.BlockSpec(memory_space=pl.ANY)
    vmem_spec = pl.BlockSpec(memory_space=pltpu.VMEM)
    shapes = []
    for which in MATRICES:
        shape = (whole[which].shape[-2], whole[which].shape[0] * whole[which].shape[-1])
        if which == FFN_IN:
            shape = (GROUP,) + shape
        shapes.append(jax.ShapeDtypeStruct(shape, full))
    results = pl.pallas_call(
        partial(backward_kernel, sizes, chunks, flat_room),
        out_shape=[jax.ShapeDtypeStruct((16, 128), full)]
        + shapes
        + [jax.ShapeDtypeStruct(rows.shape, full), jax.ShapeDtypeStruct(enc.shape, full)],
        in_specs=[any_spec, vmem_spec, vmem_spec] + [any_spec] * (2 + len(SAVED) + len(MATRICES)),
        out_specs=[vmem_spec] * (1 + len(MATRICES)) + [any_spec] * 2,
        scratch_shapes=[
            pltpu.VMEM((POOL, amount, width), low),
            pltpu.VMEM((2, amount, width), full),
            pltpu.VMEM((amount, width), full),
            pltpu.VMEM((16, width), full),
            pltpu.VMEM((16, width), full),
            pltpu.VMEM((1, hidden_units), full),
            pltpu.VMEM(sizes + (16, 128), full),
            pltpu.VMEM((amount, buckets_wide), full),
            pltpu.VMEM((2, amount, amount // 2), full),
            pltpu.VMEM((2, amount, max(amount, enc.shape[0])), full),
            pltpu.VMEM((2, amount, max(amount, enc.shape[0])), low),
            pltpu.VMEM((2,) + sizes + (ROWS, WIDE), low),
            pltpu.VMEM(whole[FFN_OUT].shape, low),
            pltpu.VMEM((2,) + kept[SELF_P].shape[1:], low),
            pltpu.VMEM((2,) + kept[CROSS_P].shape[1:], low),
            pltpu.VMEM((3,) + sizes + (ROWS, WIDE), low),
            pltpu.VMEM((2, far, near, wide_rows, tall_wide), low),
            pltpu.VMEM((flat_room, far, near, side, ROWS, WIDE), low),
        ]
        + inbox
        + [
            pltpu.SemaphoreType.DMA((32,)),
            pltpu.SemaphoreType.DMA((2 * GROUP + 1,)),
            pltpu.SemaphoreType.DMA((2,)),
            pltpu.SemaphoreType.DMA((2,)),
            pltpu.SemaphoreType.DMA((1 + enc.shape[0] // amount,)),
            pltpu.SemaphoreType.REGULAR,
            pltpu.SemaphoreType.DMA((6,)),
            pltpu.SemaphoreType.DMA((6,)),
            pltpu.SemaphoreType.DMA((total, places)),
            pltpu.SemaphoreType.DMA((total, places)),
        ],
        compiler_params=pltpu.CompilerParams(
            collective_id=1,
            has_side_effects=True,
            vmem_limit_bytes=63 * 1024 * 1024,
            fuse_transposed_lhs_in_matmul=True,
        ),
        cost_estimate=pl.CostEstimate(flops=2 * 10**10, bytes_accessed=1 << 27, transcendentals=0),
        name="backward_all",
    )(
        cotangent,
        buckets,
        valid,
        rows,
        enc,
        *[kept[name] for name in SAVED],
        *[whole[name] for name in MATRICES],
    )
    return results[0], results[1 : 1 + len(MATRICES)], results[-2], results[-1]


def finish_kernel(count, *refs):
    ins, outs, sem = refs[:count], refs[count : 2 * count], refs[2 * count]
    copies = [pltpu.make_async_copy(ins[one], outs[one], sem.at[one]) for one in range(count)]
    for one in copies:
        one.start()
    for one in copies:
        one.wait()


def finish(arrays):
    return pl.pallas_call(
        partial(finish_kernel, len(arrays)),
        out_shape=[jax.ShapeDtypeStruct(array.shape, array.dtype) for array in arrays],
        in_specs=[pl.BlockSpec(memory_space=pl.ANY)] * len(arrays),
        out_specs=[pl.BlockSpec(memory_space=pltpu.VMEM)] * len(arrays),
        scratch_shapes=[pltpu.SemaphoreType.DMA((len(arrays),))],
        name="finish",
    )(*arrays)


def quarters(sizes, block):
    split = block.reshape(block.shape[0], sizes[0] * sizes[1], GROUP, -1)
    return split.transpose(2, 0, 1, 3).reshape(GROUP, block.shape[0], -1)


def own_index():
    return lax.axis_index(AXES[0]) * lax.psum(1, AXES[1]) + lax.axis_index(AXES[1])


def spread_small(params):
    lane = lax.broadcasted_iota(jnp.int32, (1, 128), 1)
    index = own_index()
    rows = []
    for names in (VECTORS,) + tuple((name,) for name in NARROW[len(VECTORS) :]):
        width = params[names[0]].shape[0]
        fits = 128 // width
        block = jnp.tile(jnp.stack([params[name] for name in names]), (1, fits))
        rows.append(jnp.where(lane // width == lax.rem(index, fits), block, 0))
    rows.append(jnp.zeros((16 - len(NARROW), 128), rows[0].dtype))
    return jnp.concatenate(rows)


def deliver(pairs, sums):
    grads = dict(sums)
    for name in MATRICES:
        grads[name] = product_left(*pairs[name])
    return tuple(
        lax.psum_scatter(grads[name], AXES, scatter_dimension=0, tiled=True) for name in WHOLE
    )


def product(left, right):
    return jnp.dot(left, right, preferred_element_type=jnp.float32)


def product_left(left, right):
    return lax.dot_general(
        left, right, (((0,), (0,)), ((), ())), preferred_element_type=jnp.float32
    )


def product_right(left, right):
    return lax.dot_general(
        left, right, (((1,), (1,)), ((), ())), preferred_element_type=jnp.float32
    )


def column_sum(grad):
    return jnp.sum(grad.astype(jnp.float32), axis=0)


def layer_norm(summed, gain, shift):
    center = summed - jnp.mean(summed, axis=-1, keepdims=True)
    spread = jnp.mean(center * center, axis=-1, keepdims=True)
    return center * lax.rsqrt(spread + 1e-05) * gain.astype(jnp.float32) + shift.astype(jnp.float32)


def norm_back(summed, gain, shift, grad):
    unused, pull = jax.vjp(layer_norm, summed, gain.astype(jnp.float32), shift.astype(jnp.float32))
    return pull(grad)


def visible(target):
    place = jnp.arange(2 * target, dtype=jnp.int32) % target
    stream = jnp.arange(2 * target, dtype=jnp.int32) // target
    row_place = place[:, None]
    key_place = place[None, :]
    row_stream = stream[:, None]
    key_stream = stream[None, :]
    earlier = (key_stream == 0) & (
        (row_stream == 0) & (key_place <= row_place) | (row_stream == 1) & (key_place < row_place)
    )
    itself = (key_stream == 1) & (row_stream == 1) & (key_place == row_place)
    return earlier | itself


def valid_rows(lengths, target):
    valid = (jnp.arange(target, dtype=jnp.int32)[None, :] < lengths[:, None]).astype(jnp.float32)
    return jnp.concatenate([valid, valid], axis=1).reshape(-1)


def bucket_table(buckets):
    count, streams, target, width = buckets.shape
    flat = buckets.reshape(count, streams * target, width)
    return (
        flat[:, :, None, :] == jnp.arange(BUCKETS, dtype=jnp.int32)[None, None, :, None]
    ).astype(jnp.float32)


def relative_bias(onehot, relative):
    table = relative.reshape(onehot.shape[0], onehot.shape[1], -1, BUCKETS)
    return jnp.einsum("nqbk,nqhb->nhqk", onehot, table, precision=lax.Precision.HIGHEST)


def scores_of(query, keys, bias, allowed):
    scores = (
        jnp.einsum("nqhd,nkhd->nhqk", query, keys, preferred_element_type=jnp.float32) * 0.125
        + bias
    )
    return jnp.where(allowed, scores, -1e30)


def attend(query, keys, values, bias, allowed):
    scores = scores_of(query, keys, bias, allowed)
    top = jnp.max(scores, axis=-1, keepdims=True)
    logsum = top + jnp.log(jnp.sum(jnp.exp(scores - top), axis=-1, keepdims=True))
    probs = jnp.exp(scores - logsum).astype(jnp.bfloat16)
    mixed = jnp.einsum("nhqk,nkhd->nqhd", probs, values, preferred_element_type=jnp.float32)
    return (mixed.astype(jnp.bfloat16), logsum)


def attend_back(query, keys, values, bias, allowed, logsum, grad_out):
    probs = jnp.exp(scores_of(query, keys, bias, allowed) - logsum)
    grad_probs = jnp.einsum("nqhd,nkhd->nhqk", grad_out, values, preferred_element_type=jnp.float32)
    grad_scores = (
        probs * (grad_probs - jnp.sum(probs * grad_probs, axis=-1, keepdims=True))
    ).astype(jnp.bfloat16)
    grad_query = (
        jnp.einsum("nhqk,nkhd->nqhd", grad_scores, keys, preferred_element_type=jnp.float32) * 0.125
    ).astype(jnp.bfloat16)
    grad_keys = (
        jnp.einsum("nhqk,nqhd->nkhd", grad_scores, query, preferred_element_type=jnp.float32)
        * 0.125
    ).astype(jnp.bfloat16)
    grad_values = jnp.einsum(
        "nhqk,nqhd->nkhd", probs.astype(jnp.bfloat16), grad_out, preferred_element_type=jnp.float32
    ).astype(jnp.bfloat16)
    return (grad_scores, grad_query, grad_keys, grad_values)


def forward(whole, tokens, encoded, buckets):
    (
        self_q,
        self_qb,
        self_k,
        self_v,
        self_vb,
        self_o,
        self_ob,
        bucket_w,
        bucket_b,
        cross_q,
        cross_qb,
        cross_k,
        cross_v,
        cross_vb,
        cross_o,
        cross_ob,
        ffn_in,
        ffn_inb,
        ffn_out,
        ffn_outb,
        gain_a,
        shift_a,
        gain_b,
        shift_b,
        gain_c,
        shift_c,
    ) = whole
    count, streams, target, width = tokens.shape
    source = encoded.shape[1]
    head_shape = (count, streams * target, width // HEAD_DIM, HEAD_DIM)
    source_shape = (count, source, width // HEAD_DIM, HEAD_DIM)
    rows = tokens.reshape(-1, width)
    enc_rows = encoded.reshape(-1, width)
    allowed = visible(target)
    query = (product(rows, self_q) + self_qb).astype(jnp.bfloat16)
    keys = product(rows, self_k).astype(jnp.bfloat16)
    values = (product(rows, self_v) + self_vb).astype(jnp.bfloat16)
    relative = product(rows, bucket_w) + bucket_b
    bias = relative_bias(bucket_table(buckets), relative)
    mixed, logsum = attend(
        query.reshape(head_shape),
        keys.reshape(head_shape),
        values.reshape(head_shape),
        bias,
        allowed,
    )
    mixed = mixed.reshape(rows.shape)
    sum_first = rows + product(mixed, self_o) + self_ob
    first = layer_norm(sum_first, gain_a, shift_a)
    first_low = first.astype(jnp.bfloat16)
    probe = (product(first_low, cross_q) + cross_qb).astype(jnp.bfloat16)
    index = product(enc_rows, cross_k).astype(jnp.bfloat16)
    content = (product(enc_rows, cross_v) + cross_vb).astype(jnp.bfloat16)
    joined, cross_logsum = attend(
        probe.reshape(head_shape),
        index.reshape(source_shape),
        content.reshape(source_shape),
        0.0,
        True,
    )
    joined = joined.reshape(rows.shape)
    sum_second = first + product(joined, cross_o) + cross_ob
    second = layer_norm(sum_second, gain_b, shift_b)
    second_low = second.astype(jnp.bfloat16)
    before = product(second_low, ffn_in) + ffn_inb
    activity = jax.nn.gelu(before, approximate=False).astype(jnp.bfloat16)
    sum_third = second + product(activity, ffn_out) + ffn_outb
    third = layer_norm(sum_third, gain_c, shift_c)
    kept = (
        rows,
        enc_rows,
        query,
        keys,
        values,
        relative,
        logsum,
        mixed,
        sum_first,
        first_low,
        probe,
        index,
        content,
        cross_logsum,
        joined,
        sum_second,
        second_low,
        before,
        activity,
        sum_third,
    )
    return (third, kept)


def backward(whole, kept, cotangent, buckets, lengths):
    (
        self_q,
        self_qb,
        self_k,
        self_v,
        self_vb,
        self_o,
        self_ob,
        bucket_w,
        bucket_b,
        cross_q,
        cross_qb,
        cross_k,
        cross_v,
        cross_vb,
        cross_o,
        cross_ob,
        ffn_in,
        ffn_inb,
        ffn_out,
        ffn_outb,
        gain_a,
        shift_a,
        gain_b,
        shift_b,
        gain_c,
        shift_c,
    ) = whole
    (
        rows,
        enc_rows,
        query,
        keys,
        values,
        relative,
        logsum,
        mixed,
        sum_first,
        first_low,
        probe,
        index,
        content,
        cross_logsum,
        joined,
        sum_second,
        second_low,
        before,
        activity,
        sum_third,
    ) = kept
    count, streams, target, width = cotangent.shape
    source = enc_rows.shape[0] // count
    head_shape = (count, streams * target, width // HEAD_DIM, HEAD_DIM)
    source_shape = (count, source, width // HEAD_DIM, HEAD_DIM)
    allowed = visible(target)
    grad_third = (
        cotangent.reshape(rows.shape).astype(jnp.float32) * valid_rows(lengths, target)[:, None]
    )
    grad_sum_third, grad_gain_c, grad_shift_c = norm_back(sum_third, gain_c, shift_c, grad_third)
    branch_three = grad_sum_third.astype(jnp.bfloat16)
    pair_ffn_out = (activity, branch_three)
    grad_ffn_outb = column_sum(branch_three)
    unused, gelu_pull = jax.vjp(partial(jax.nn.gelu, approximate=False), before)
    grad_before = gelu_pull(product_right(branch_three, ffn_out))[0].astype(jnp.bfloat16)
    pair_ffn_in = (second_low, grad_before)
    grad_ffn_inb = column_sum(grad_before)
    grad_second = grad_sum_third + product_right(grad_before, ffn_in)
    grad_sum_second, grad_gain_b, grad_shift_b = norm_back(sum_second, gain_b, shift_b, grad_second)
    branch_two = grad_sum_second.astype(jnp.bfloat16)
    pair_cross_o = (joined, branch_two)
    grad_cross_ob = column_sum(branch_two)
    grad_joined = product_right(branch_two, cross_o).astype(jnp.bfloat16)
    unused, grad_probe, grad_index, grad_content = attend_back(
        probe.reshape(head_shape),
        index.reshape(source_shape),
        content.reshape(source_shape),
        0.0,
        True,
        cross_logsum,
        grad_joined.reshape(head_shape),
    )
    grad_probe = grad_probe.reshape(rows.shape)
    grad_index = grad_index.reshape(enc_rows.shape)
    grad_content = grad_content.reshape(enc_rows.shape)
    pair_cross_q = (first_low, grad_probe)
    grad_cross_qb = column_sum(grad_probe)
    pair_cross_k = (enc_rows, grad_index)
    pair_cross_v = (enc_rows, grad_content)
    grad_cross_vb = column_sum(grad_content)
    grad_encoded = product_right(grad_index, cross_k) + product_right(grad_content, cross_v)
    grad_first = grad_sum_second + product_right(grad_probe, cross_q)
    grad_sum_first, grad_gain_a, grad_shift_a = norm_back(sum_first, gain_a, shift_a, grad_first)
    branch_one = grad_sum_first.astype(jnp.bfloat16)
    pair_self_o = (mixed, branch_one)
    grad_self_ob = column_sum(branch_one)
    grad_mixed = product_right(branch_one, self_o).astype(jnp.bfloat16)
    onehot = bucket_table(buckets)
    bias = relative_bias(onehot, relative)
    grad_scores, grad_query, grad_keys, grad_values = attend_back(
        query.reshape(head_shape),
        keys.reshape(head_shape),
        values.reshape(head_shape),
        bias,
        allowed,
        logsum,
        grad_mixed.reshape(head_shape),
    )
    grad_relative = jnp.einsum(
        "nqbk,nhqk->nqhb", onehot, grad_scores.astype(jnp.float32), precision=lax.Precision.HIGHEST
    )
    grad_relative = grad_relative.reshape(rows.shape[0], -1).astype(jnp.bfloat16)
    grad_query = grad_query.reshape(rows.shape)
    grad_keys = grad_keys.reshape(rows.shape)
    grad_values = grad_values.reshape(rows.shape)
    pair_self_q = (rows, grad_query)
    grad_self_qb = column_sum(grad_query)
    pair_self_k = (rows, grad_keys)
    pair_self_v = (rows, grad_values)
    grad_self_vb = column_sum(grad_values)
    pair_bucket_w = (rows, grad_relative)
    grad_bucket_b = column_sum(grad_relative)
    grad_tokens = (
        grad_sum_first
        + product_right(grad_query, self_q)
        + product_right(grad_keys, self_k)
        + product_right(grad_values, self_v)
        + product_right(grad_relative, bucket_w)
    )
    pairs = (
        pair_self_q,
        pair_self_k,
        pair_self_v,
        pair_bucket_w,
        pair_self_o,
        pair_cross_k,
        pair_cross_v,
        pair_cross_q,
        pair_cross_o,
        pair_ffn_in,
        pair_ffn_out,
    )
    sums = (
        grad_self_qb,
        grad_self_vb,
        grad_self_ob,
        grad_cross_qb,
        grad_cross_vb,
        grad_cross_ob,
        grad_ffn_outb,
        grad_gain_a,
        grad_shift_a,
        grad_gain_b,
        grad_shift_b,
        grad_gain_c,
        grad_shift_c,
        grad_bucket_b,
        grad_ffn_inb,
    )
    return (
        dict(zip(MATRICES, pairs)),
        dict(zip(NARROW, sums)),
        grad_tokens.reshape(cotangent.shape),
        grad_encoded.reshape(count, source, width),
    )


def per_device(mesh_shape, tokens, encoded, cotangent, buckets, lengths, *shards):
    params = dict(zip(WHOLE, shards))
    dp, fsdp = mesh_shape
    sizes = chips(dp, fsdp)
    valid = valid_rows(lengths, tokens.shape[2])[:, None]
    if any(params[name].shape[0] % ROWS for name in MATRICES):
        whole = tuple(lax.all_gather(params[name], AXES, axis=0, tiled=True) for name in WHOLE)
        third, kept = forward(whole, tokens, encoded, buckets)
        outputs = (third * valid).astype(jnp.bfloat16)
        pairs, sums, grad_tokens, grad_encoded = backward(whole, kept, cotangent, buckets, lengths)
        shares = deliver(pairs, sums)
    else:
        rows = tokens.reshape(-1, tokens.shape[-1])
        enc_rows = encoded.reshape(-1, encoded.shape[-1])
        table = buckets.reshape(rows.shape[0], -1)
        outputs, whole, kept = forward_all(
            sizes,
            spread_small(params),
            [
                quarters(sizes, params[name]) if name == FFN_IN else params[name]
                for name in MATRICES
            ],
            rows,
            enc_rows,
            table,
            valid,
        )
        small, own, grad_tokens, grad_encoded = backward_all(
            sizes, whole, kept, rows, enc_rows, cotangent.reshape(rows.shape), table, valid
        )
        plain = [one for one, name in zip(own, MATRICES) if name != FFN_IN]
        outputs, grad_tokens, grad_encoded, *plain = finish(
            [outputs, grad_tokens, grad_encoded] + plain
        )
        out = dict(zip([name for name in MATRICES if name != FFN_IN], plain))
        grad = own[MATRICES.index(FFN_IN)]
        grad = grad.reshape(GROUP, grad.shape[1], sizes[0] * sizes[1], -1)
        out[FFN_IN] = grad.transpose(1, 2, 0, 3).reshape(params[FFN_IN].shape)
        index = own_index()
        for row, name in enumerate(NARROW):
            width = params[name].shape[0]
            at = lax.rem(index, 128 // width) * width
            out[name] = lax.dynamic_slice(small, (row, at), (1, width)).reshape(width)
        shares = tuple(out[name] for name in WHOLE)
    return (
        outputs.reshape(tokens.shape),
        grad_tokens.reshape(tokens.shape),
        grad_encoded.reshape(encoded.shape),
    ) + shares


def solution(mesh):
    def split(ranks):
        return tuple(P(AXES, *[None] * (rank - 1)) for rank in ranks)

    ranks = tuple(1 if name in NARROW else 2 for name in WHOLE)
    return jax.shard_map(
        partial(per_device, (mesh.shape[AXES[0]], mesh.shape[AXES[1]])),
        mesh=mesh,
        in_specs=split((4, 3, 4, 4, 1) + ranks),
        out_specs=split((4, 4, 3) + ranks),
        check_vma=False,
    )
```
